256 devices in a mesh: seq: 8 (over x, core), state: 32 (over z, y).
Axes of the slice: x: 4, y: 4, z: 8, core: 2. Of those that a mesh axis runs over, the one named last changes fastest.
Arguments:
- alpha_in: float32 [256, 131072], P('seq', 'state'), may hold values from 0.1 to 3
- beta_in: float32 [256, 131072], P('seq', 'state'), may hold values from 0.1 to 3
- transitions: bfloat16 [1024, 4, 128, 128], P('state'), may hold values from 0.049804688 to 1
- emission_cols: bfloat16 [256, 131072], P(None, 'state'), may hold values from 0.049804688 to 1
- token_ids: int32 [256, 4], P('seq'), may hold values from 0 to 255
- sources: int32 [1024, 4], replicated, may hold values from 0 to 1023, as said below
Outputs:
- counts: float32 [1024, 4, 128, 128], P('state', None, 'seq')
- alpha_end: float32 [256, 131072], P('seq', 'state')
- beta_start: float32 [256, 131072], P('seq', 'state')
- loglik: float32 [256], P('seq')
The draws below stay inside these ranges and needn't reach their ends.
Inputs may be any that keep to these rules, and one draw needn't show every extreme that they name: `sources`: block b lies with index b // 32 of state. The 128 entries of the rows of one index of state name blocks of exactly 16 distinct indices, exactly 8 entries for each of them; which indices is drawn, and the same block may be named more than once.
All inputs are finite; a program needn't handle non-finite values.
Results may differ from the reference program's by a relative error of at most 0.0016.
Values may be sent and summed in bfloat16 or wider, within the bound.
A program may use at most 128 MiB of HBM per device.

```python
import math
import jax
import jax.numpy as jnp
from jax import lax

BS = 128
K = 4
BLK_DEV = 32
STEPS = 4
V_WIN = 256
STATES = 131072
NB = 1024
SEQS = 256
N_STATE = 32


def draw_sources(key, part):
    key = jax.random.fold_in(key, 7)
    peer_count = NB // BLK_DEV
    ref_count = BLK_DEV * K
    group_count = peer_count // 2
    capacity = ref_count // group_count

    def one_device(device_key, device_number):
        first_key, second_key, third_key = jax.random.split(device_key, 3)
        shuffled = jax.random.permutation(first_key, peer_count).astype(jnp.int32)
        target = jnp.where(device_number == 0, 0, peer_count - 1).astype(jnp.int32)
        extreme = jnp.where(device_number == 0, 0, BLK_DEV - 1).astype(jnp.int32)
        position = jnp.sum(jnp.where(shuffled == target, jnp.arange(peer_count, dtype=jnp.int32), 0)).astype(jnp.int32)
        leading = shuffled[0]
        shuffled = shuffled.at[position].set(leading).at[0].set(target)
        owners = shuffled[:group_count]
        placing = jax.random.permutation(second_key, ref_count)
        owner_of = owners[placing // capacity]
        local_index = jax.random.randint(third_key, (ref_count,), 0, BLK_DEV).astype(jnp.int32)
        local_index = jnp.where(placing == 0, extreme, local_index)
        return (owner_of * BLK_DEV + local_index).astype(jnp.int32)
    device_keys = jax.random.split(key, peer_count)
    numbers = jnp.arange(peer_count, dtype=jnp.int32)
    return jax.vmap(one_device)(device_keys, numbers).reshape(NB, K)


def plant(values, rng, low, top_value):
    longest = values.shape.index(max(values.shape))
    spots = []
    for shift in (0, 1):
        where = [jax.random.randint(jax.random.fold_in(rng, axis), (), 0, length) for axis, length in enumerate(values.shape)]
        where[longest] = (where[longest] + shift) % values.shape[longest]
        spots.append(tuple(where))
    return values.at[spots[0]].set(low).at[spots[1]].set(top_value)


def level_of(stream_key, dims, cuts, low, largest):
    def one(dim, shards_of):
        heights = jax.random.uniform(jax.random.fold_in(jax.random.fold_in(stream_key, 6), dim), (shards_of,), jnp.float32, low / len(cuts), largest / len(cuts))
        return jnp.repeat(jnp.exp(heights), dims[dim] // shards_of).reshape((-1,) + (1,) * (len(dims) - dim - 1))

    loudness = one(*cuts[0])
    for cut in cuts[1:]:
        loudness = loudness * one(*cut)
    return loudness


def setup_inputs(seed: int = 0) -> dict:
    splits = jax.random.split(jax.random.key(seed), 7)
    alpha_in = jnp.clip(jnp.exp(math.log(3.0) - 3.4011974 * jax.random.uniform(splits[0], (SEQS, STATES), jnp.float32) ** level_of(splits[0], (SEQS, STATES), ((0, 8), (1, 32)), -0.2, 0.2)), 0.1, 3.0)
    beta_in = jnp.clip(jnp.exp(math.log(3.0) - 3.4011974 * jax.random.uniform(splits[1], (SEQS, STATES), jnp.float32) ** level_of(splits[1], (SEQS, STATES), ((0, 8), (1, 32)), -0.2, 0.2)), 0.1, 3.0)
    transitions = jnp.clip(jnp.exp(math.log(1.0) - 2.9996462 * jax.random.uniform(splits[2], (NB, K, BS, BS), jnp.float32) ** level_of(splits[2], (NB, K, BS, BS), ((0, 32),), -0.2, 0.2)), 0.049804688, 1.0).astype(jnp.bfloat16)
    emission_cols = jnp.clip(jnp.exp(math.log(1.0) - 2.9996462 * jax.random.uniform(splits[3], (V_WIN, STATES), jnp.float32) ** level_of(splits[3], (V_WIN, STATES), ((1, 32),), -0.2, 0.2)), 0.049804688, 1.0).astype(jnp.bfloat16)
    token_ids = plant(jax.random.randint(splits[4], (SEQS, STEPS), 0, V_WIN), jax.random.fold_in(splits[4], 1), 0, V_WIN - 1).astype(jnp.int32)
    sources = draw_sources(jax.random.fold_in(splits[6], 71), 0)
    return {"alpha_in": alpha_in, "beta_in": beta_in, "transitions": transitions, "emission_cols": emission_cols, "token_ids": token_ids, "sources": sources}


def reference(alpha_in, beta_in, transitions, emission_cols, token_ids, sources):
    seq_count = alpha_in.shape[0]
    source_groups = sources.reshape(N_STATE, BLK_DEV, K)
    trans_groups = transitions.reshape(N_STATE, BLK_DEV, K, BS, BS)
    forward = alpha_in
    loglik = jnp.zeros((seq_count,), jnp.float32)
    history = []
    for position in range(STEPS):
        emission = jnp.take(emission_cols, token_ids[:, position], axis=0).astype(jnp.float32)
        outgoing = forward.astype(jnp.bfloat16).reshape(seq_count, NB, BS)

        def forward_piece(pair, outgoing=outgoing):
            group_src, group_trans = pair
            fetched = outgoing[:, group_src.reshape(-1)].reshape(seq_count, BLK_DEV, K, BS)
            return jnp.einsum("sjka,jkab->sjb", fetched.astype(jnp.float32), group_trans.astype(jnp.float32))

        mixture = lax.map(forward_piece, (source_groups, trans_groups))
        mixture = jnp.transpose(mixture, (1, 0, 2, 3)).reshape(seq_count, STATES)
        scaled = emission * mixture
        factor = jnp.sum(scaled, axis=1) / STATES
        loglik = loglik + jnp.log(factor)
        history.append((outgoing, scaled))
        forward = scaled / factor[:, None]
    backward = beta_in
    counts = jnp.zeros((N_STATE, BLK_DEV, K, BS, BS), jnp.float32)
    for position in reversed(range(STEPS)):
        outgoing, scaled = history[position]
        emission = jnp.take(emission_cols, token_ids[:, position], axis=0).astype(jnp.float32)
        weighted = emission * backward
        pair_mean = jnp.sum(scaled * backward, axis=1) / STATES
        posterior = (weighted / pair_mean[:, None]).astype(jnp.bfloat16).reshape(seq_count, N_STATE, BLK_DEV, BS)
        spread = weighted.astype(jnp.bfloat16).reshape(seq_count, N_STATE, BLK_DEV, BS)

        def count_piece(items, outgoing=outgoing):
            group_src, group_post = items
            fetched = outgoing[:, group_src.reshape(-1)].reshape(seq_count, BLK_DEV, K, BS)
            return jnp.einsum("sjka,sjb->jkab", fetched.astype(jnp.float32), group_post.astype(jnp.float32))

        counts = counts + lax.map(count_piece, (source_groups, jnp.transpose(posterior, (1, 0, 2, 3))))

        def return_piece(carry, items):
            group_src, group_trans, group_spread = items
            partial_value = jnp.einsum("sjb,jkab->sjka", group_spread.astype(jnp.float32), group_trans.astype(jnp.float32)).astype(jnp.bfloat16)
            partial_value = lax.optimization_barrier(partial_value).astype(jnp.float32)
            carry = carry.at[:, group_src.reshape(-1)].add(partial_value.reshape(seq_count, BLK_DEV * K, BS))
            return carry, None

        raw_beta, unused_out = lax.scan(return_piece, jnp.zeros((seq_count, NB, BS), jnp.float32),
                                        (source_groups, trans_groups, jnp.transpose(spread, (1, 0, 2, 3))))
        raw_beta = raw_beta.reshape(seq_count, STATES)
        factor = jnp.sum(raw_beta, axis=1) / STATES
        backward = raw_beta / factor[:, None]
    counts = counts.reshape(NB, K, BS, BS) * transitions.astype(jnp.float32)
    return counts, forward, backward, loglik
```

```python
import jax
import jax.numpy as jnp
from jax import lax
from jax.sharding import PartitionSpec as P

K = 4
STEPS = 4


def shards(alpha_in, beta_in, transitions, emission_cols, token_ids, sources):
    seq_count = alpha_in.shape[0]
    local_width = alpha_in.shape[1]
    blocks = transitions.shape[0]
    block_size = transitions.shape[2]
    peer_count = lax.axis_size("state")
    rank_here = lax.axis_index("state")
    ref_count = blocks * K
    groups = peer_count // 2
    capacity = ref_count // groups
    states_total = local_width * peer_count
    own_source = lax.dynamic_slice_in_dim(sources, rank_here * blocks, blocks, 0).reshape(ref_count)
    own_owner = own_source // blocks
    ordinal = jnp.arange(ref_count, dtype=jnp.int32)
    earlier = (own_owner[None, :] == own_owner[:, None]) & (ordinal[None, :] < ordinal[:, None])
    own_slot = jnp.sum(earlier.astype(jnp.int32), axis=1)
    all_owner = sources.reshape(peer_count, ref_count) // blocks
    all_local = sources.reshape(peer_count, ref_count) % blocks
    from_here = all_owner == rank_here
    slot_all = jnp.cumsum(from_here.astype(jnp.int32), axis=1) - 1
    chosen = from_here[:, :, None] & (
        slot_all[:, :, None] == jnp.arange(capacity, dtype=jnp.int32)[None, None, :]
    )
    send_index = jnp.sum(jnp.where(chosen, all_local[:, :, None], 0), axis=1)
    filled = jnp.any(chosen, axis=1)
    collect = (
        (send_index[:, :, None] == jnp.arange(blocks, dtype=jnp.int32)[None, None, :])
        & filled[:, :, None]
    ).astype(jnp.bfloat16)
    emissions = [
        jnp.take(emission_cols, token_ids[:, position], axis=0).astype(jnp.float32)
        for position in range(STEPS)
    ]
    forward = alpha_in
    backward = beta_in
    fetched_all = [None] * STEPS
    weighted_all = [None] * STEPS
    for step in range(STEPS):
        outgoing = forward.astype(jnp.bfloat16)
        fetch_parcel = jnp.take(outgoing.reshape(seq_count, blocks, block_size), send_index, axis=1)
        arrived = lax.all_to_all(fetch_parcel, "state", split_axis=1, concat_axis=1, tiled=True)
        fetched = arrived[:, own_owner, own_slot].reshape(seq_count, blocks, K, block_size)
        fetched_all[step] = fetched
        mixture = jnp.einsum(
            "sjka,jkab->sjb", fetched, transitions, preferred_element_type=jnp.float32
        ).reshape(seq_count, local_width)
        forward = emissions[step] * mixture

        position = STEPS - 1 - step
        weighted = (emissions[position] * backward).astype(jnp.bfloat16)
        spread = weighted.reshape(seq_count, blocks, block_size)
        weighted_all[position] = spread
        partial_value = jnp.einsum(
            "sjb,jkab->sjka", spread, transitions, preferred_element_type=jnp.float32
        )
        partial_value = partial_value.astype(jnp.bfloat16).reshape(seq_count, ref_count, block_size)
        parcel = jnp.zeros((seq_count, peer_count, capacity, block_size), jnp.bfloat16)
        parcel = parcel.at[:, own_owner, own_slot].set(partial_value)
        returned = lax.all_to_all(parcel, "state", split_axis=1, concat_axis=1, tiled=True)
        backward = jnp.einsum(
            "sxca,xcb->sba", returned, collect, preferred_element_type=jnp.float32
        ).reshape(seq_count, local_width)
    ends = jnp.stack([jnp.sum(forward, axis=1), jnp.sum(forward * beta_in, axis=1)])
    ends = lax.psum(ends, "state") / states_total
    back_mean = lax.psum(jnp.sum(partial_value.astype(jnp.float32), axis=(1, 2)), "state") / states_total
    pair = ends[1]
    fetched = jnp.concatenate(fetched_all, axis=0)
    posterior = jnp.concatenate(
        [(w / pair[:, None, None]).astype(jnp.bfloat16) for w in weighted_all], axis=0
    )
    counts = jnp.einsum("sjka,sjb->jkab", fetched, posterior, preferred_element_type=jnp.float32)
    counts = counts * transitions.astype(jnp.float32)
    shares = lax.psum_scatter(counts, "seq", scatter_dimension=2, tiled=True)
    return (
        shares,
        forward / ends[0][:, None],
        backward / back_mean[:, None],
        jnp.log(ends[0]),
    )


def solution(mesh):
    placed = (
        P("seq", "state"),
        P("seq", "state"),
        P("state", None, None, None),
        P(None, "state"),
        P("seq", None),
        P(),
    )
    return jax.shard_map(
        shards,
        mesh=mesh,
        in_specs=placed,
        out_specs=(P("state", None, "seq", None), P("seq", "state"), P("seq", "state"), P("seq")),
        check_vma=False,
    )
```

```python
import functools

import jax
import jax.numpy as jnp
from jax import lax
from jax.experimental import pallas as pl
from jax.experimental.pallas import tpu as pltpu
from jax.sharding import PartitionSpec as P

K = 4
STEPS = 4
NZ = 8
NY = 4
CAP = 8
NB = 32
NS = 32
BS = 128
REFS = NB * K
COL = NZ * CAP
CHUNK = 8
MESH = pl.DeviceIdType.MESH
F32 = jnp.float32
BF16 = jnp.bfloat16

SEL, REF, INV, ORD, LO, HI = 0, 256, 384, 640, 896, 1152


def index_tables(sources):
    rank = lax.axis_index("state")
    z, y = rank // NY, rank % NY
    rows = lax.dynamic_slice_in_dim(sources.reshape(NZ, NY * REFS), z, 1, 0).reshape(NY, REFS)
    rows = jnp.roll(rows, -y, axis=0)
    owner, local = rows // NB, rows % NB
    ordinal = jnp.arange(REFS, dtype=jnp.int32)
    earlier = (owner[:, None, :] == owner[:, :, None]) & (ordinal[None, :] < ordinal[:, None])[None]
    slot = jnp.sum(earlier.astype(jnp.int32), axis=2)
    place = (owner // NY) * CAP + slot
    column = owner % NY
    spots = jnp.arange(COL, dtype=jnp.int32)
    mine = (column == y)[:, :, None] & (place[:, :, None] == spots)
    sel = jnp.sum(jnp.where(mine, local[:, :, None], 0), axis=1)
    filled = jnp.any(mine, axis=1)
    ref = ((y - column[0]) % NY) * COL + place[0]
    towards = ((column[0] - y) % NY) * COL + place[0]
    inv = jnp.sum(
        jnp.where(towards[:, None] == jnp.arange(NY * COL, dtype=jnp.int32), ordinal[:, None], 0), axis=0
    )
    key = jnp.where(filled, sel, NB)
    key = jnp.concatenate([key[:1], key[:0:-1]], axis=0).reshape(NY, NZ, CAP)
    key = key.transpose(1, 0, 2).reshape(NZ, NY * CAP)
    number = jnp.arange(NY * CAP, dtype=jnp.int32)
    less = (key[:, None, :] < key[:, :, None]) | (
        (key[:, None, :] == key[:, :, None]) & (number[None, :] < number[:, None])[None]
    )
    rank_of = jnp.sum(less.astype(jnp.int32), axis=2)
    home = (number // CAP) * COL + number % CAP
    home = home[None, :] + jnp.arange(NZ, dtype=jnp.int32)[:, None] * CAP
    order = jnp.sum(jnp.where(rank_of[:, :, None] == number, home[:, :, None], 0), axis=1)
    blocks = jnp.arange(NB, dtype=jnp.int32)
    low = jnp.sum((key[:, None, :] < blocks[None, :, None]).astype(jnp.int32), axis=2)
    high = jnp.sum((key[:, None, :] <= blocks[None, :, None]).astype(jnp.int32), axis=2)
    return jnp.concatenate([part.reshape(-1).astype(jnp.int32) for part in (sel, ref, inv, order, low, high)])


def body(
    tab, alpha, beta, tr, em,
    counts, alpha_end, beta_start, loglik,
    zg0, zg1, yr0, yr1, yr2, yr3, ys, pb, bsend, br0, br1, pre, psv,
    rs_snd, rs_rcv, rl_snd, rl_rcv, w, bacc, cs, cr, sa, sb, sc, sd, scale,
    ag_s, ag_r, bw_s, bw_r, fw_s, fw_r, rs_s, rs_r, sy_s, sy_r, sz_s, sz_r, ct_s, ct_r,
):
    q, p = lax.axis_index("seq"), lax.axis_index("state")
    z, y = p // NY, p % NY
    zgs, yrs, brs = (zg0, zg1), (yr0, yr1, yr2, yr3), (br0, br1)
    total_states = float(NB * BS * NZ * NY)

    def at_z(dz):
        return (q, lax.rem(z + dz + NZ, NZ) * NY + y)

    def at_y(dy):
        return (q, z * NY + lax.rem(y + dy, NY))

    def at_q(dq):
        return (lax.rem(q + dq, 8), p)

    barrier = pltpu.get_barrier_semaphore()
    for dz in range(1, NZ):
        pl.semaphore_signal(barrier, inc=1, device_id=at_z(dz), device_id_type=MESH)
    for dy in range(1, NY):
        pl.semaphore_signal(barrier, inc=1, device_id=at_y(dy), device_id_type=MESH)
    for dq in range(1, 8):
        pl.semaphore_signal(barrier, inc=1, device_id=at_q(dq), device_id_type=MESH)
    pl.semaphore_wait(barrier, NZ - 1 + NY - 1 + 7)

    def remote(src, dst, send, recv, device):
        return pltpu.make_async_remote_copy(
            src_ref=src, dst_ref=dst, send_sem=send, recv_sem=recv, device_id=device, device_id_type=MESH
        )

    def cols(j):
        return pl.ds(pl.multiple_of(j * BS, BS), BS)

    def gather_copy(r, way, h):
        zg = zgs[r % 2]
        near, far = (h - 1, h) if way else ((1 - h) % NZ, (-h) % NZ)
        src, dst = zg.at[near], zg.at[far]
        if h == 4:
            half = pl.ds(way * 16, 16)
            src, dst = zg.at[near, half], zg.at[far, half]
        return remote(src, dst, ag_s.at[r, way, h - 1], ag_r.at[r, way, h - 1], at_z(-1 if way else 1))

    def reduce_copy(r, way, h):
        snd, rcv = (rl_snd, rl_rcv) if r == 3 else (rs_snd, rs_rcv)
        src, dst = snd.at[way, h - 1], rcv.at[way, h - 1]
        if h == 1:
            half = pl.ds(way * 16, 16)
            src, dst = snd.at[way, 0, half], rcv.at[way, 0, half]
        return remote(src, dst, rs_s.at[r, way, h - 1], rs_r.at[r, way, h - 1], at_z(-1 if way else 1))

    def back_copy(r, dy):
        return remote(
            bsend.at[dy - 1], brs[r % 2].at[pl.ds(dy * COL, COL)], bw_s.at[r, dy - 1], bw_r.at[r, dy - 1], at_y(dy)
        )

    def fetch_copy(r, dy):
        return remote(
            ys.at[dy - 1], yrs[r].at[pl.ds(dy * COL, COL)], fw_s.at[r, dy - 1], fw_r.at[r, dy - 1], at_y(dy)
        )

    def sum_y_copy(n, dy):
        return remote(sa.at[n], sb.at[n, dy - 1], sy_s.at[n, dy - 1], sy_r.at[n, dy - 1], at_y(dy))

    def sum_z_copy(n, dz):
        return remote(sc.at[n], sd.at[n, dz - 1], sz_s.at[n, dz - 1], sz_r.at[n, dz - 1], at_z(dz))

    def counts_copy(c, dq):
        piece = pl.ds(c * CHUNK, CHUNK)
        return remote(
            cs.at[lax.rem(q + dq, 8), piece], cr.at[dq - 1, piece], ct_s.at[c, dq - 1], ct_r.at[c, dq - 1], at_q(dq)
        )

    def sum_over_y(n):
        for dy in range(1, NY):
            sum_y_copy(n, dy).start()

    def sum_over_z(n):
        for dy in range(1, NY):
            sum_y_copy(n, dy).wait()
        sc[n] = sa[n] + sb[n, 0] + sb[n, 1] + sb[n, 2]
        for dz in range(1, NZ):
            sum_z_copy(n, dz).start()

    def sum_result(n):
        for dz in range(1, NZ):
            sum_z_copy(n, dz).wait()
        total = sc[n]
        for dz in range(1, NZ):
            total = total + sd[n, dz - 1]
        return jnp.sum(total, axis=2, keepdims=True) / total_states

    def weigh(r):
        u = STEPS - 1 - r

        def step(b, carry):
            message = beta[:, cols(b)] if r == 0 else bacc[b]
            if r == 3:
                message = message * scale[1]
            w[u, b] = (em[u, :, cols(b)].astype(F32) * message).astype(BF16)
            return carry

        lax.fori_loop(0, NB, step, 0)

    def partials(r):
        u = STEPS - 1 - r

        def step(j, acc):
            out = lax.dot_general(w[u, j], tr[j], (((1,), (1,)), ((), ())), preferred_element_type=F32)
            for k in range(K):
                piece = out[:, k * BS : (k + 1) * BS]
                pb[j * K + k] = piece.astype(BF16)
                if r >= 2:
                    acc = acc + piece
            return acc

        return lax.fori_loop(0, NB, step, jnp.zeros((NS, BS), F32))

    def relay(r, d):
        br = brs[r % 2]
        base = lax.rem(z + d + NZ, NZ) * NB
        pre[0] = jnp.zeros((NS, BS), F32)

        def add(i, acc):
            acc = acc + br[tab[ORD + base + i]].astype(F32)
            pre[i + 1] = acc
            return acc

        lax.fori_loop(0, NB, add, jnp.zeros((NS, BS), F32))

        def differ(b, carry):
            psv[d % NZ, b] = pre[tab[HI + base + b]] - pre[tab[LO + base + b]]
            return carry

        lax.fori_loop(0, NB, differ, 0)

    def begin(b, carry):
        zg0[0, b] = alpha[:, cols(b)].astype(BF16)
        return carry

    lax.fori_loop(0, NB, begin, 0)

    for r in range(STEPS):
        zg, yr, br = zgs[r % 2], yrs[r], brs[r % 2]
        for way in range(2):
            gather_copy(r, way, 1).start()
        weigh(r)
        acc = partials(r)
        if r >= 2:
            sa[r - 2, 1] = acc
        if r == 2:
            sum_over_y(0)
        for dy in (1, 3, 2):

            def pack(i, carry, dy=dy):
                bsend[dy - 1, i] = pb[tab[INV + dy * COL + i]]
                return carry

            lax.fori_loop(0, COL, pack, 0)
            back_copy(r, dy).start()

        def keep(i, carry):
            br[i] = pb[tab[INV + i]]
            return carry

        lax.fori_loop(0, COL, keep, 0)
        for h in range(2, 5):
            for way in range(2):
                gather_copy(r, way, h - 1).wait_recv()
                gather_copy(r, way, h).start()
        for way in range(2):
            gather_copy(r, way, 4).wait_recv()

        for dy in (1, 3, 2):

            def choose(i, carry, dy=dy):
                d = lax.rem(i // CAP - z + NZ, NZ)
                ys[dy - 1, i] = zg[d, tab[SEL + dy * COL + i]]
                return carry

            lax.fori_loop(0, COL, choose, 0)
            fetch_copy(r, dy).start()

        def hold(i, carry):
            d = lax.rem(i // CAP - z + NZ, NZ)
            yr[i] = zg[d, tab[SEL + i]]
            return carry

        lax.fori_loop(0, COL, hold, 0)
        for way in range(2):
            for h in range(1, 5):
                gather_copy(r, way, h).wait_send()
        for dy in range(1, NY):
            back_copy(r, dy).wait()
        if r == 2:
            sum_over_z(0)

        snd, rcv = (rl_snd, rl_rcv) if r == 3 else (rs_snd, rs_rcv)
        kind = snd.dtype
        relay(r, 4)

        def far(b, carry):
            snd[0, 0, b] = psv[4, b].astype(kind)
            snd[1, 0, b + 16] = psv[4, b + 16].astype(kind)
            return carry

        lax.fori_loop(0, 16, far, 0)
        for way in range(2):
            reduce_copy(r, way, 1).start()
        for h in range(2, 5):
            d = 5 - h
            relay(r, d)
            relay(r, -d)
            for way in range(2):
                reduce_copy(r, way, h - 1).wait_recv()
                dd = (-d if way else d) % NZ
                if h == 2:

                    def join(b, carry, way=way, dd=dd):
                        there, other = b + way * 16, b + (1 - way) * 16
                        snd[way, 1, there] = (psv[dd, there] + rcv[way, 0, there].astype(F32)).astype(kind)
                        snd[way, 1, other] = psv[dd, other].astype(kind)
                        return carry

                    lax.fori_loop(0, 16, join, 0)
                else:

                    def join(b, carry, way=way, dd=dd, h=h):
                        snd[way, h - 1, b] = (psv[dd, b] + rcv[way, h - 2, b].astype(F32)).astype(kind)
                        return carry

                    lax.fori_loop(0, NB, join, 0)
                reduce_copy(r, way, h).start()
        relay(r, 0)
        if r < 3:
            for way in range(2):
                reduce_copy(r, way, 4).wait_recv()

            def finish(b, carry):
                bacc[b] = psv[0, b] + rcv[0, 3, b].astype(F32) + rcv[1, 3, b].astype(F32)
                return carry

            lax.fori_loop(0, NB, finish, 0)
            for way in range(2):
                for h in range(1, 5):
                    reduce_copy(r, way, h).wait_send()
        if r == 2:
            means = sum_result(0)
            scale[0] = jnp.broadcast_to(1.0 / means[0], (NS, BS))
            scale[1] = jnp.broadcast_to(1.0 / means[1], (NS, BS))
            scale[2] = jnp.broadcast_to(means[1] / means[0], (NS, BS))

        for dy in range(1, NY):
            fetch_copy(r, dy).wait()

        def mix(j, acc):
            x = jnp.concatenate([yr[tab[REF + j * K + k]] for k in range(K)], axis=1)
            value = jnp.dot(x, tr[j], preferred_element_type=F32) * em[r, :, cols(j)].astype(F32)
            if r == 3:
                alpha_end[:, cols(j)] = value
                return acc + value
            zgs[(r + 1) % 2][0, j] = value.astype(BF16)
            if r == 1:
                acc = acc + value * bacc[j]
            return acc

        acc = lax.fori_loop(0, NB, mix, jnp.zeros((NS, BS), F32))
        if r == 1:
            sa[0, 0] = acc
        if r == 3:
            sa[1, 0] = acc
            sum_over_y(1)

    for c in range(NB // CHUNK):

        def tally(i, carry, c=c):
            j = c * CHUNK + i
            x = jnp.concatenate(
                [jnp.concatenate([v[tab[REF + j * K + k]] for k in range(K)], axis=1) for v in yrs], axis=0
            )
            weights = jnp.concatenate(
                [(w[t, j].astype(F32) * scale[2 if t == 0 else 0]).astype(BF16) for t in range(STEPS)], axis=0
            )
            out = lax.dot_general(x, weights, (((0,), (0,)), ((), ())), preferred_element_type=F32).astype(BF16)
            for k in range(K):
                for part in range(8):
                    first = k * BS + part * 16
                    cs[part, j, k] = out[first : first + 16]
            return carry

        lax.fori_loop(0, CHUNK, tally, 0)
        for dq in range(1, 8):
            counts_copy(c, dq).start()
        if c == 0:
            sum_over_z(1)

    for way in range(2):
        reduce_copy(3, way, 4).wait_recv()
    means = sum_result(1)
    start_scale = jnp.broadcast_to(1.0 / means[1], (NS, BS))
    end_scale = jnp.broadcast_to(1.0 / means[0], (NS, BS))
    loglik[...] = jnp.broadcast_to(jnp.log(means[0]), (NS, BS))

    def last(b, carry):
        beta_start[:, cols(b)] = (psv[0, b] + rl_rcv[0, 3, b] + rl_rcv[1, 3, b]) * start_scale
        alpha_end[:, cols(b)] = alpha_end[:, cols(b)] * end_scale
        return carry

    lax.fori_loop(0, NB, last, 0)
    for way in range(2):
        for h in range(1, 5):
            reduce_copy(3, way, h).wait_send()

    for c in range(NB // CHUNK):
        for dq in range(1, 8):
            counts_copy(c, dq).wait()

        def total(i, carry, c=c):
            j = c * CHUNK + i
            value = cs[q, j].astype(F32)
            for dq in range(1, 8):
                value = value + cr[dq - 1, j].astype(F32)
            for k in range(K):
                rows = pl.ds(pl.multiple_of(k * BS + q * 16, 16), 16)
                counts[j, k] = value[k] * tr[j, rows, :].astype(F32)
            return carry

        lax.fori_loop(0, CHUNK, total, 0)


def shards(alpha_in, beta_in, transitions, emission_cols, token_ids, sources):
    tables = index_tables(sources)
    em = jnp.take(emission_cols, token_ids.T, axis=0)
    shard = (NB, NS, BS)
    vmem = pl.BlockSpec(memory_space=pltpu.VMEM)
    dma = pltpu.SemaphoreType.DMA
    out = pl.pallas_call(
        body,
        out_shape=(
            jax.ShapeDtypeStruct((NB, K, BS // 8, BS), F32),
            jax.ShapeDtypeStruct((NS, NB * BS), F32),
            jax.ShapeDtypeStruct((NS, NB * BS), F32),
            jax.ShapeDtypeStruct((NS, BS), F32),
        ),
        in_specs=[pl.BlockSpec(memory_space=pltpu.SMEM)] + [vmem] * 4,
        out_specs=(vmem,) * 4,
        scratch_shapes=[
            pltpu.VMEM((NZ,) + shard, BF16),
            pltpu.VMEM((NZ,) + shard, BF16),
            *[pltpu.VMEM((NY * COL, NS, BS), BF16)] * STEPS,
            pltpu.VMEM((NY - 1, COL, NS, BS), BF16),
            pltpu.VMEM((REFS, NS, BS), BF16),
            pltpu.VMEM((NY - 1, COL, NS, BS), BF16),
            pltpu.VMEM((NY * COL, NS, BS), BF16),
            pltpu.VMEM((NY * COL, NS, BS), BF16),
            pltpu.VMEM((NB + 1, NS, BS), F32),
            pltpu.VMEM((NZ,) + shard, F32),
            pltpu.VMEM((2, 4) + shard, BF16),
            pltpu.VMEM((2, 4) + shard, BF16),
            pltpu.VMEM((2, 4) + shard, F32),
            pltpu.VMEM((2, 4) + shard, F32),
            pltpu.VMEM((STEPS,) + shard, BF16),
            pltpu.VMEM(shard, F32),
            pltpu.VMEM((8, NB, K, BS // 8, BS), BF16),
            pltpu.VMEM((7, NB, K, BS // 8, BS), BF16),
            pltpu.VMEM((2, 2, NS, BS), F32),
            pltpu.VMEM((2, NY - 1, 2, NS, BS), F32),
            pltpu.VMEM((2, 2, NS, BS), F32),
            pltpu.VMEM((2, NZ - 1, 2, NS, BS), F32),
            pltpu.VMEM((3, NS, BS), F32),
            *[dma((STEPS, 2, 4))] * 2,
            *[dma((STEPS, NY - 1))] * 4,
            *[dma((STEPS, 2, 4))] * 2,
            *[dma((2, NY - 1))] * 2,
            *[dma((2, NZ - 1))] * 2,
            *[dma((NB // CHUNK, 7))] * 2,
        ],
        compiler_params=pltpu.CompilerParams(
            collective_id=0, has_side_effects=True, vmem_limit_bytes=62 * 2**20
        ),
        cost_estimate=pl.CostEstimate(flops=1_700_000_000, bytes_accessed=10_000_000, transcendentals=32),
    )(tables, alpha_in, beta_in, transitions.reshape(NB, K * BS, BS), em)
    return out[0], out[1], out[2], out[3][:, 0]


def solution(mesh):
    placed = (
        P("seq", "state"),
        P("seq", "state"),
        P("state", None, None, None),
        P(None, "state"),
        P("seq", None),
        P(),
    )
    return jax.shard_map(
        shards,
        mesh=mesh,
        in_specs=placed,
        out_specs=(P("state", None, "seq", None), P("seq", "state"), P("seq", "state"), P("seq")),
        check_vma=False,
    )
```

```python
import functools

import jax
import jax.numpy as jnp
from jax import lax
from jax.experimental import pallas as pl
from jax.experimental.pallas import tpu as pltpu
from jax.sharding import PartitionSpec as P

K = 4
STEPS = 4
NZ = 8
NY = 4
NX = 4
CAP = 8
NB = 32
NS = 32
BS = 128
REFS = NB * K
COL = NZ * CAP
CHUNK = 8
PIECES = 4
PIECE = NB // PIECES
TURNS = (4, 3, 5, 2, 6, 1, 7, 0)
EARLY = 5
MESH = pl.DeviceIdType.MESH
F32 = jnp.float32
BF16 = jnp.bfloat16

SEL, REF, INV, ORD, LO, HI = 0, 256, 384, 640, 896, 1152


def index_tables(sources):
    rank = lax.axis_index("state")
    z, y = rank // NY, rank % NY
    rows = lax.dynamic_slice_in_dim(sources.reshape(NZ, NY * REFS), z, 1, 0).reshape(NY, REFS)
    rows = jnp.roll(rows, -y, axis=0)
    owner, local = rows // NB, rows % NB
    ordinal = jnp.arange(REFS, dtype=jnp.int32)
    earlier = (owner[:, None, :] == owner[:, :, None]) & (ordinal[None, :] < ordinal[:, None])[None]
    slot = jnp.sum(earlier.astype(jnp.int32), axis=2)
    ahead = (owner // NY - z) % NZ
    column = owner % NY
    place = ahead * CAP + slot
    spots = jnp.arange(COL, dtype=jnp.int32)
    mine = (column == y)[:, :, None] & (place[:, :, None] == spots)
    sel = jnp.sum(jnp.where(mine, local[:, :, None], 0), axis=1)
    filled = jnp.any(mine, axis=1)
    ref = ((y - column[0]) % NY) * COL + place[0]
    turn = jnp.where(ahead[0] <= 4, jnp.maximum(7 - 2 * ahead[0], 0), 2 * ahead[0] - 8)
    towards = ((column[0] - y) % NY) * COL + turn * CAP + slot[0]
    inv = jnp.sum(
        jnp.where(towards[:, None] == jnp.arange(NY * COL, dtype=jnp.int32), ordinal[:, None], 0), axis=0
    )
    key = jnp.where(filled, sel, NB)
    key = jnp.concatenate([key[:1], key[:0:-1]], axis=0).reshape(NY, NZ, CAP)
    key = key.transpose(1, 0, 2).reshape(NZ, NY * CAP)
    key = jnp.stack([key[d] for d in TURNS])
    number = jnp.arange(NY * CAP, dtype=jnp.int32)
    less = (key[:, None, :] < key[:, :, None]) | (
        (key[:, None, :] == key[:, :, None]) & (number[None, :] < number[:, None])[None]
    )
    rank_of = jnp.sum(less.astype(jnp.int32), axis=2)
    order = jnp.sum(jnp.where(rank_of[:, :, None] == number, number[None, :, None], 0), axis=1)
    blocks = jnp.arange(NB, dtype=jnp.int32)
    low = jnp.sum((key[:, None, :] < blocks[None, :, None]).astype(jnp.int32), axis=2)
    high = jnp.sum((key[:, None, :] <= blocks[None, :, None]).astype(jnp.int32), axis=2)
    return jnp.concatenate([part.reshape(-1).astype(jnp.int32) for part in (sel, ref, inv, order, low, high)])


def loop(count, fn, init=0, width=1):
    def several(i, carry):
        return fn([i * width + n for n in range(width)], carry)

    several.__name__ = fn.__name__
    return lax.fori_loop(0, count // width, several, init)


def body(
    tab, alpha, beta, tr, em,
    counts, alpha_end, beta_start, loglik,
    zg0, zg1, yr0, yr1, yr2, yr3, ys, pb, bsend, br0, br1, bs0, bs1, pre, psv,
    rs_snd, rs_rcv, rl_rcv, w, bacc, cs, cp, cx, cr, sa, sb, sc, sd, scale,
    ag_s, ag_r, bw_s, bw_r, fw_s, fw_r, rs_s, rs_r, sy_s, sy_r, sz_s, sz_r, cp_s, cp_r, ct_s, ct_r,
):
    q, p = lax.axis_index("seq"), lax.axis_index("state")
    z, y = p // NY, p % NY
    x, core = q // 2, q % 2
    zgs, yrs, brs = (zg0, zg1), (yr0, yr1, yr2, yr3), ((br0, bs0), (br1, bs1))
    total_states = float(NB * BS * NZ * NY)

    def at_z(dz):
        return (q, lax.rem(z + dz + NZ, NZ) * NY + y)

    def at_y(dy):
        return (q, z * NY + lax.rem(y + dy, NY))

    def at_x(dx):
        return (lax.rem(x + dx, NX) * 2 + core, p)

    partner = (x * 2 + 1 - core, p)

    barrier = pltpu.get_barrier_semaphore()
    for dz in range(1, NZ):
        pl.semaphore_signal(barrier, inc=1, device_id=at_z(dz), device_id_type=MESH)
    for dy in range(1, NY):
        pl.semaphore_signal(barrier, inc=1, device_id=at_y(dy), device_id_type=MESH)
    for dx in range(1, NX):
        pl.semaphore_signal(barrier, inc=1, device_id=at_x(dx), device_id_type=MESH)
    pl.semaphore_signal(barrier, inc=1, device_id=partner, device_id_type=MESH)

    def remote(src, dst, send, recv, device):
        return pltpu.make_async_remote_copy(
            src_ref=src, dst_ref=dst, send_sem=send, recv_sem=recv, device_id=device, device_id_type=MESH
        )

    def cols(j):
        return pl.ds(pl.multiple_of(j * BS, BS), BS)

    def part(c):
        return pl.ds(c * PIECE, PIECE)

    def travels(way, c):
        return c // (PIECES // 2) == way

    def gather_copy(r, way, h, c):
        zg = zgs[r % 2]
        near, far = (h - 1, h) if way else ((1 - h) % NZ, (-h) % NZ)
        return remote(
            zg.at[near, part(c)], zg.at[far, part(c)],
            ag_s.at[r, way, h - 1, c], ag_r.at[r, way, h - 1, c], at_z(-1 if way else 1),
        )

    def reduce_copy(r, way, h, c):
        if r == 3 and h >= 3:
            d = (h - 5 if way else 5 - h) % NZ
            src, dst = psv.at[d, part(c)], rl_rcv.at[way, h - 3, part(c)]
        else:
            src = rs_snd.at[part(c)] if h == 1 else rs_rcv.at[way, h - 2, part(c)]
            dst = rs_rcv.at[way, h - 1, part(c)]
        return remote(src, dst, rs_s.at[r, way, h - 1, c], rs_r.at[r, way, h - 1, c], at_z(-1 if way else 1))

    def back_copy(r, dy, late):
        src = bsend.at[dy - 1, pl.ds(EARLY, NZ - EARLY) if late else pl.ds(0, EARLY)]
        dst = brs[r % 2][late].at[:, pl.ds(dy * CAP, CAP)]
        return remote(src, dst, bw_s.at[r, late, dy - 1], bw_r.at[r, late, dy - 1], at_y(dy))

    def fetch_copy(r, dy):
        return remote(
            ys.at[dy - 1], yrs[r].at[pl.ds(dy * COL, COL)], fw_s.at[r, dy - 1], fw_r.at[r, dy - 1], at_y(dy)
        )

    def sum_y_copy(n, dy):
        return remote(sa.at[n], sb.at[n, dy - 1], sy_s.at[n, dy - 1], sy_r.at[n, dy - 1], at_y(dy))

    def sum_z_copy(n, dz):
        return remote(sc.at[n], sd.at[n, dz - 1], sz_s.at[n, dz - 1], sz_r.at[n, dz - 1], at_z(dz))

    def core_copy(c):
        piece = pl.ds(c * CHUNK, CHUNK)
        return remote(cs.at[1 - core, :, piece], cp.at[:, piece], cp_s.at[c], cp_r.at[c], partner)

    def counts_copy(c, dx):
        piece = pl.ds(c * CHUNK, CHUNK)
        return remote(
            cx.at[lax.rem(x + dx, NX), piece], cr.at[dx - 1, piece], ct_s.at[c, dx - 1], ct_r.at[c, dx - 1], at_x(dx)
        )

    def sum_over_y(n):
        for dy in range(1, NY):
            sum_y_copy(n, dy).start()

    def sum_over_z(n):
        for dy in range(1, NY):
            sum_y_copy(n, dy).wait()
        sc[n] = sa[n] + sb[n, 0] + sb[n, 1] + sb[n, 2]
        for dz in range(1, NZ):
            sum_z_copy(n, dz).start()

    def sum_result(n):
        for dz in range(1, NZ):
            sum_z_copy(n, dz).wait()
        total = sc[n]
        for dz in range(1, NZ):
            total = total + sd[n, dz - 1]
        return jnp.sum(total, axis=2, keepdims=True) / total_states

    def weigh(r):
        u = STEPS - 1 - r

        def weigh_block(blocks, carry):
            for b in blocks:
                message = beta[:, cols(b)] if r == 0 else bacc[b]
                if r == 3:
                    message = message * scale[1]
                w[u, b] = (em[u, :, cols(b)].astype(F32) * message).astype(BF16)
            return carry

        loop(NB, weigh_block, 0, 4)

    def partials(r):
        u = STEPS - 1 - r

        def partial_block(js, acc):
            outs = [
                lax.dot_general(w[u, j], tr[j], (((1,), (1,)), ((), ())), preferred_element_type=F32) for j in js
            ]
            for j, out in zip(js, outs):
                for k in range(K):
                    piece = out[:, k * BS : (k + 1) * BS]
                    pb[j * K + k] = piece.astype(BF16)
                    if r >= 2:
                        acc = acc + piece
            return acc

        acc = loop(NB, partial_block, jnp.zeros((NS, BS), F32), 4)
        if r >= 2:
            sa[r - 2, 1] = acc

    def send_back(r):
        for late in range(2):
            first, past = (EARLY, NZ) if late else (0, EARLY)
            for dy in (1, 3, 2):

                def pack(turns, carry, dy=dy):
                    for n in turns:
                        base = INV + dy * COL + n * CAP
                        values = [pb[tab[base + c]] for c in range(CAP)]
                        for c in range(CAP):
                            bsend[dy - 1, n, c] = values[c]
                    return carry

                lax.fori_loop(first, past, lambda n, carry, pack=pack: pack([n], carry), 0)
                back_copy(r, dy, late).start()

            def keep(turns, carry, late=late, first=first):
                for n in turns:
                    base = INV + n * CAP
                    values = [pb[tab[base + c]] for c in range(CAP)]
                    for c in range(CAP):
                        brs[r % 2][late][n - first, c] = values[c]
                return carry

            lax.fori_loop(first, past, lambda n, carry, keep=keep: keep([n], carry), 0)

    def relay(r, d):
        turn = TURNS.index(d % NZ)
        late = int(turn >= EARLY)
        br, place = brs[r % 2][late], turn - EARLY * late
        base = turn * NB
        pre[0] = jnp.zeros((NS, BS), F32)

        def add(numbers, acc):
            terms = [br[place, tab[ORD + base + i]] for i in numbers]
            for i, term in zip(numbers, terms):
                acc = acc + term.astype(F32)
                pre[i + 1] = acc
            return acc

        loop(NB, add, jnp.zeros((NS, BS), F32), 8)

        def differ(blocks, carry):
            values = [pre[tab[HI + base + b]] - pre[tab[LO + base + b]] for b in blocks]
            for b, value in zip(blocks, values):
                psv[d % NZ, b] = value
            return carry

        loop(NB, differ, 0, 4)

    def mix(r, c, acc):
        yr = yrs[r]

        def mix_block(numbers, acc):
            js = [c * PIECE + i for i in numbers]
            fetched = [jnp.concatenate([yr[tab[REF + j * K + k]] for k in range(K)], axis=1) for j in js]
            outs = [jnp.dot(f, tr[j], preferred_element_type=F32) for f, j in zip(fetched, js)]
            for j, out in zip(js, outs):
                value = out * em[r, :, cols(j)].astype(F32)
                if r == 3:
                    alpha_end[:, cols(j)] = value
                    acc = acc + value
                else:
                    zgs[(r + 1) % 2][0, j] = value.astype(BF16)
                    if r == 1:
                        acc = acc + value * bacc[j]
            return acc

        return loop(PIECE, mix_block, acc, 4)

    for c in range(PIECES):

        def begin(i, carry, c=c):
            b = c * PIECE + i
            zg0[0, b] = alpha[:, cols(b)].astype(BF16)
            return carry

        lax.fori_loop(0, PIECE, begin, 0)
        if c == 0:
            pl.semaphore_wait(barrier, NZ - 1 + NY - 1 + NX)
        for way in range(2):
            gather_copy(0, way, 1, c).start()
    weigh(0)
    partials(0)
    send_back(0)

    for r in range(STEPS):
        zg, yr = zgs[r % 2], yrs[r]
        for h in range(2, 5):
            for c in range(PIECES):
                for way in range(2):
                    gather_copy(r, way, h - 1, c).wait_recv()
                    if h < 4 or travels(way, c):
                        gather_copy(r, way, h, c).start()
        for c in range(PIECES):
            gather_copy(r, 0 if travels(0, c) else 1, 4, c).wait_recv()

        for dy in range(1, NY):
            back_copy(r, dy, 0).wait()
        relay(r, 4)

        def far(blocks, carry):
            for b in blocks:
                rs_snd[b] = psv[4, b].astype(BF16)
            return carry

        loop(NB, far, 0, 4)
        for c in range(PIECES):
            reduce_copy(r, 0 if travels(0, c) else 1, 1, c).start()
        for dy in (1, 3, 2):

            def choose(ds, carry, dy=dy):
                for d in ds:
                    base = SEL + dy * COL + d * CAP
                    values = [zg[d, tab[base + c]] for c in range(CAP)]
                    for c in range(CAP):
                        ys[dy - 1, d * CAP + c] = values[c]
                return carry

            loop(NZ, choose, 0, 1)
            fetch_copy(r, dy).start()

        def hold(ds, carry):
            for d in ds:
                base = SEL + d * CAP
                values = [zg[d, tab[base + c]] for c in range(CAP)]
                for c in range(CAP):
                    yr[d * CAP + c] = values[c]
            return carry

        loop(NZ, hold, 0, 1)
        if r == 2:
            sum_over_z(0)
        for h in range(2, 5):
            if h == 4:
                for dy in range(1, NY):
                    back_copy(r, dy, 1).wait()
            for way in range(2):
                relay(r, h - 5 if way else 5 - h)
            for c in range(PIECES):
                for way in range(2):
                    d = (h - 5 if way else 5 - h) % NZ
                    received = h > 2 or travels(way, c)
                    if received:
                        reduce_copy(r, way, h - 1, c).wait_recv()

                    def join(numbers, carry, way=way, d=d, h=h, c=c, received=received):
                        for b in [c * PIECE + i for i in numbers]:
                            value = psv[d, b]
                            if r == 3 and h == 4:
                                psv[d, b] = value + rl_rcv[way, 0, b]
                                continue
                            if received:
                                value = value + rs_rcv[way, h - 2, b].astype(F32)
                            if r == 3 and h == 3:
                                psv[d, b] = value
                            else:
                                rs_rcv[way, h - 2, b] = value.astype(BF16)
                        return carry

                    loop(PIECE, join, 0, 4)
                    reduce_copy(r, way, h, c).start()
        relay(r, 0)
        for way in range(2):
            for h in range(1, 5):
                for c in range(PIECES):
                    if h < 4 or travels(way, c):
                        gather_copy(r, way, h, c).wait_send()
        if r < 3:
            for c in range(PIECES):
                for way in range(2):
                    reduce_copy(r, way, 4, c).wait_recv()

                def finish(numbers, carry, c=c):
                    for b in [c * PIECE + i for i in numbers]:
                        bacc[b] = psv[0, b] + rs_rcv[0, 3, b].astype(F32) + rs_rcv[1, 3, b].astype(F32)
                    return carry

                loop(PIECE, finish, 0, 4)
            for way in range(2):
                for h in range(1, 5):
                    for c in range(PIECES):
                        if h > 1 or travels(way, c):
                            reduce_copy(r, way, h, c).wait_send()
            if r == 2:
                means = sum_result(0)
                scale[0] = jnp.broadcast_to(1.0 / means[0], (NS, BS))
                scale[1] = jnp.broadcast_to(1.0 / means[1], (NS, BS))
                scale[2] = jnp.broadcast_to(means[1] / means[0], (NS, BS))
            weigh(r + 1)
            partials(r + 1)
        for dy in range(1, NY):
            fetch_copy(r, dy).wait()
        if r < 3:
            send_back(r + 1)

        if r < 3:
            acc = jnp.zeros((NS, BS), F32)
            for c in range(PIECES):
                acc = mix(r, c, acc)
                for way in range(2):
                    gather_copy(r + 1, way, 1, c).start()
        if r == 1:
            sa[0, 0] = acc
            sum_over_y(0)

    def merge(c):
        core_copy(c).wait()

        def merge_block(i, carry):
            j = c * CHUNK + i
            for xp in range(NX):
                cx[xp, j] = (cs[core, xp, j] + cp[xp, j]).astype(BF16)
            return carry

        lax.fori_loop(0, CHUNK, merge_block, 0)
        for dx in range(1, NX):
            counts_copy(c, dx).start()

    for c in range(NB // CHUNK):

        def tally(i, carry, c=c):
            j = c * CHUNK + i
            left = jnp.concatenate(
                [jnp.concatenate([v[tab[REF + j * K + k]] for k in range(K)], axis=1) for v in yrs], axis=0
            )
            right = jnp.concatenate(
                [(w[t, j].astype(F32) * scale[2 if t == 0 else 0]).astype(BF16) for t in range(STEPS)], axis=0
            )
            out = lax.dot_general(left, right, (((0,), (0,)), ((), ())), preferred_element_type=F32)
            for k in range(K):
                for n in range(8):
                    first = k * BS + n * 16
                    cs[n % 2, n // 2, j, k] = out[first : first + 16]
            return carry

        lax.fori_loop(0, CHUNK, tally, 0)
        core_copy(c).start()
        if c > 0:
            merge(c - 1)
    merge(NB // CHUNK - 1)

    acc = jnp.zeros((NS, BS), F32)
    for c in range(PIECES):
        acc = mix(3, c, acc)
    sa[1, 0] = acc
    sum_over_y(1)
    sum_over_z(1)
    means = sum_result(1)
    start_scale = jnp.broadcast_to(1.0 / means[1], (NS, BS))
    end_scale = jnp.broadcast_to(1.0 / means[0], (NS, BS))
    loglik[...] = jnp.broadcast_to(jnp.log(means[0]), (NS, BS))
    for c in range(PIECES):
        for way in range(2):
            reduce_copy(3, way, 4, c).wait_recv()

        def last(i, carry, c=c):
            b = c * PIECE + i
            beta_start[:, cols(b)] = (psv[0, b] + rl_rcv[0, 1, b] + rl_rcv[1, 1, b]) * start_scale
            alpha_end[:, cols(b)] = alpha_end[:, cols(b)] * end_scale
            return carry

        lax.fori_loop(0, PIECE, last, 0)
    for way in range(2):
        for h in range(1, 5):
            for c in range(PIECES):
                if h > 1 or travels(way, c):
                    reduce_copy(3, way, h, c).wait_send()

    for c in range(NB // CHUNK):
        for dx in range(1, NX):
            counts_copy(c, dx).wait()

        def total(i, carry, c=c):
            j = c * CHUNK + i
            value = cs[core, x, j] + cp[x, j]
            for dx in range(1, NX):
                value = value + cr[dx - 1, j].astype(F32)
            for k in range(K):
                rows = pl.ds(pl.multiple_of(k * BS + q * 16, 16), 16)
                counts[j, k] = value[k] * tr[j, rows, :].astype(F32)
            return carry

        lax.fori_loop(0, CHUNK, total, 0)


def shards(alpha_in, beta_in, transitions, emission_cols, token_ids, sources):
    tables = index_tables(sources)
    em = jnp.take(emission_cols, token_ids.T, axis=0)
    shard = (NB, NS, BS)
    vmem = pl.BlockSpec(memory_space=pltpu.VMEM)
    dma = pltpu.SemaphoreType.DMA
    out = pl.pallas_call(
        body,
        out_shape=(
            jax.ShapeDtypeStruct((NB, K, BS // 8, BS), F32),
            jax.ShapeDtypeStruct((NS, NB * BS), F32),
            jax.ShapeDtypeStruct((NS, NB * BS), F32),
            jax.ShapeDtypeStruct((NS, BS), F32),
        ),
        in_specs=[pl.BlockSpec(memory_space=pltpu.SMEM)] + [vmem] * 4,
        out_specs=(vmem,) * 4,
        scratch_shapes=[
            pltpu.VMEM((NZ,) + shard, BF16),
            pltpu.VMEM((NZ,) + shard, BF16),
            *[pltpu.VMEM((NY * COL, NS, BS), BF16)] * STEPS,
            pltpu.VMEM((NY - 1, COL, NS, BS), BF16),
            pltpu.VMEM((REFS, NS, BS), BF16),
            pltpu.VMEM((NY - 1, NZ, CAP, NS, BS), BF16),
            *[pltpu.VMEM((EARLY, NY * CAP, NS, BS), BF16)] * 2,
            *[pltpu.VMEM((NZ - EARLY, NY * CAP, NS, BS), BF16)] * 2,
            pltpu.VMEM((NB + 1, NS, BS), F32),
            pltpu.VMEM((NZ,) + shard, F32),
            pltpu.VMEM(shard, BF16),
            pltpu.VMEM((2, 4) + shard, BF16),
            pltpu.VMEM((2, 2) + shard, F32),
            pltpu.VMEM((STEPS,) + shard, BF16),
            pltpu.VMEM(shard, F32),
            pltpu.VMEM((2, NX, NB, K, BS // 8, BS), F32),
            pltpu.VMEM((NX, NB, K, BS // 8, BS), F32),
            pltpu.VMEM((NX, NB, K, BS // 8, BS), BF16),
            pltpu.VMEM((NX - 1, NB, K, BS // 8, BS), BF16),
            pltpu.VMEM((2, 2, NS, BS), F32),
            pltpu.VMEM((2, NY - 1, 2, NS, BS), F32),
            pltpu.VMEM((2, 2, NS, BS), F32),
            pltpu.VMEM((2, NZ - 1, 2, NS, BS), F32),
            pltpu.VMEM((3, NS, BS), F32),
            *[dma((STEPS, 2, 4, PIECES))] * 2,
            *[dma((STEPS, 2, NY - 1))] * 2,
            *[dma((STEPS, NY - 1))] * 2,
            *[dma((STEPS, 2, 4, PIECES))] * 2,
            *[dma((2, NY - 1))] * 2,
            *[dma((2, NZ - 1))] * 2,
            *[dma((NB // CHUNK,))] * 2,
            *[dma((NB // CHUNK, NX - 1))] * 2,
        ],
        compiler_params=pltpu.CompilerParams(
            collective_id=0, has_side_effects=True, vmem_limit_bytes=62 * 2**20
        ),
        cost_estimate=pl.CostEstimate(flops=1_700_000_000, bytes_accessed=10_000_000, transcendentals=32),
    )(tables, alpha_in, beta_in, transitions.reshape(NB, K * BS, BS), em)
    return out[0], out[1], out[2], out[3][:, 0]


def solution(mesh):
    placed = (
        P("seq", "state"),
        P("seq", "state"),
        P("state", None, None, None),
        P(None, "state"),
        P("seq", None),
        P(),
    )
    return jax.shard_map(
        shards,
        mesh=mesh,
        in_specs=placed,
        out_specs=(P("state", None, "seq", None), P("seq", "state"), P("seq", "state"), P("seq")),
        check_vma=False,
    )
```

```python
import functools

import jax
import jax.numpy as jnp
from jax import lax
from jax.experimental import pallas as pl
from jax.experimental.pallas import tpu as pltpu
from jax.sharding import PartitionSpec as P

K = 4
STEPS = 4
NZ = 8
NY = 4
NX = 4
CAP = 8
NB = 32
NS = 32
BS = 128
REFS = NB * K
COL = NZ * CAP
CHUNK = 8
PIECES = 4
PIECE = NB // PIECES
TURNS = (4, 3, 5, 2, 6, 1, 7, 0)
LOTS = (0, 3, 5, 7, 8)
NEAR = (0, 1, 7, 2, 6, 3, 5, 4)
GROUPS = (0, 1, 3, 5, 7, 8)
TOKENS = 256
MESH = pl.DeviceIdType.MESH
F32 = jnp.float32
BF16 = jnp.bfloat16

SEL, REF, INV, ORD, LO, HI = 0, 256, 384, 640, 896, 1152


def index_tables(sources):
    rank = lax.axis_index("state")
    z, y = rank // NY, rank % NY
    rows = lax.dynamic_slice_in_dim(sources.reshape(NZ, NY * REFS), z, 1, 0).reshape(NY, REFS)
    rows = jnp.roll(rows, -y, axis=0)
    owner, local = rows // NB, rows % NB
    ordinal = jnp.arange(REFS, dtype=jnp.int32)
    earlier = (owner[:, None, :] == owner[:, :, None]) & (ordinal[None, :] < ordinal[:, None])[None]
    slot = jnp.sum(earlier.astype(jnp.int32), axis=2)
    ahead = (owner // NY - z) % NZ
    column = owner % NY
    place = ahead * CAP + slot
    spots = jnp.arange(COL, dtype=jnp.int32)
    mine = (column == y)[:, :, None] & (place[:, :, None] == spots)
    sel = jnp.sum(jnp.where(mine, local[:, :, None], 0), axis=1)
    filled = jnp.any(mine, axis=1)
    near = jnp.where(ahead[0] <= 3, jnp.maximum(2 * ahead[0] - 1, 0), jnp.minimum(16 - 2 * ahead[0], 7))
    ref = ((y - column[0]) % NY) * COL + near * CAP + slot[0]
    turn = jnp.where(ahead[0] <= 4, jnp.maximum(7 - 2 * ahead[0], 0), 2 * ahead[0] - 8)
    towards = ((column[0] - y) % NY) * COL + turn * CAP + slot[0]
    inv = jnp.sum(
        jnp.where(towards[:, None] == jnp.arange(NY * COL, dtype=jnp.int32), ordinal[:, None], 0), axis=0
    )
    key = jnp.where(filled, sel, NB)
    key = jnp.concatenate([key[:1], key[:0:-1]], axis=0).reshape(NY, NZ, CAP)
    key = key.transpose(1, 0, 2).reshape(NZ, NY * CAP)
    key = jnp.stack([key[d] for d in TURNS])
    number = jnp.arange(NY * CAP, dtype=jnp.int32)
    less = (key[:, None, :] < key[:, :, None]) | (
        (key[:, None, :] == key[:, :, None]) & (number[None, :] < number[:, None])[None]
    )
    rank_of = jnp.sum(less.astype(jnp.int32), axis=2)
    order = jnp.sum(jnp.where(rank_of[:, :, None] == number, number[None, :, None], 0), axis=1)
    blocks = jnp.arange(NB, dtype=jnp.int32)
    low = jnp.sum((key[:, None, :] < blocks[None, :, None]).astype(jnp.int32), axis=2)
    high = jnp.sum((key[:, None, :] <= blocks[None, :, None]).astype(jnp.int32), axis=2)
    return jnp.concatenate([part.reshape(-1).astype(jnp.int32) for part in (sel, ref, inv, order, low, high)])


def loop(count, fn, init=0, width=1):
    def several(i, carry):
        return fn([i * width + n for n in range(width)], carry)

    several.__name__ = fn.__name__
    return lax.fori_loop(0, count // width, several, init)


def body(
    tab, hot, alpha_hbm, beta_hbm, tr_hbm, cols_hbm,
    counts, alpha_end, beta_start, loglik,
    za0, za1, za2, za3, za4, za5, za6, za7, zb0, zb1, zb2, zb3, zb4, zb5, zb6, zb7,
    em, yr0, yr1, yr2, yr3, ys, pb, bsend, ba0, ba1, ba2, ba3, bb0, bb1, bb2, bb3, pre, psv,
    rs_snd, rs_rcv, rl_rcv, w, bacc, cs, cp, cx, cr, sa, sp, sb, sc, sd, scale, alpha, beta, tr, cols_in, ld,
    ag_s, ag_r, bw_s, bw_r, fw_s, fw_r, rs_s, rs_r, sy_s, sy_r, sz_s, sz_r, cp_s, cp_r, ct_s, ct_r,
):
    q, p = lax.axis_index("seq"), lax.axis_index("state")
    z, y = p // NY, p % NY
    x, core = q // 2, q % 2
    zgs = (za0, za1, za2, za3, za4, za5, za6, za7), (zb0, zb1, zb2, zb3, zb4, zb5, zb6, zb7)
    yrs, brs = (yr0, yr1, yr2, yr3), ((ba0, ba1, ba2, ba3), (bb0, bb1, bb2, bb3))
    total_states = float(NB * BS * NZ * NY)

    def at_z(dz):
        return (q, lax.rem(z + dz + NZ, NZ) * NY + y)

    def at_y(dy):
        return (q, z * NY + lax.rem(y + dy, NY))

    def at_x(dx):
        return (lax.rem(x + dx, NX) * 2 + core, p)

    partner = (x * 2 + 1 - core, p)

    loads = [
        pltpu.make_async_copy(src, dst, ld.at[n])
        for n, (src, dst) in enumerate(((alpha_hbm, alpha), (cols_hbm, cols_in), (beta_hbm, beta), (tr_hbm, tr)))
    ]
    for load in loads:
        load.start()
    barrier = pltpu.get_barrier_semaphore()
    for dz in range(1, NZ):
        pl.semaphore_signal(barrier, inc=1, device_id=at_z(dz), device_id_type=MESH)
    for dy in range(1, NY):
        pl.semaphore_signal(barrier, inc=1, device_id=at_y(dy), device_id_type=MESH)
    for dx in range(1, NX):
        pl.semaphore_signal(barrier, inc=1, device_id=at_x(dx), device_id_type=MESH)
    pl.semaphore_signal(barrier, inc=1, device_id=partner, device_id_type=MESH)

    def remote(src, dst, send, recv, device):
        return pltpu.make_async_remote_copy(
            src_ref=src, dst_ref=dst, send_sem=send, recv_sem=recv, device_id=device, device_id_type=MESH
        )

    def cols(j):
        return pl.ds(pl.multiple_of(j * BS, BS), BS)

    def part(c):
        return pl.ds(c * PIECE, PIECE)

    def travels(way, c):
        return c // (PIECES // 2) == way

    def gather_copy(r, way, h, c):
        zg = zgs[r % 2]
        near, far = (h - 1, h) if way else ((1 - h) % NZ, (-h) % NZ)
        return remote(
            zg[near].at[part(c)], zg[far].at[part(c)],
            ag_s.at[r, way, h - 1, c], ag_r.at[r, way, h - 1, c], at_z(-1 if way else 1),
        )

    def reduce_copy(r, way, h, c):
        if r == 3 and h >= 3:
            d = (h - 5 if way else 5 - h) % NZ
            src, dst = psv.at[d, part(c)], rl_rcv.at[way, h - 3, part(c)]
        else:
            src = rs_snd.at[part(c)] if h == 1 else rs_rcv.at[r % 2, way, h - 2, part(c)]
            dst = rs_rcv.at[r % 2, way, h - 1, part(c)]
        return remote(src, dst, rs_s.at[r, way, h - 1, c], rs_r.at[r, way, h - 1, c], at_z(-1 if way else 1))

    def back_copy(r, dy, lot):
        src = bsend.at[dy - 1, pl.ds(LOTS[lot], LOTS[lot + 1] - LOTS[lot])]
        dst = brs[r % 2][lot].at[:, pl.ds(dy * CAP, CAP)]
        return remote(src, dst, bw_s.at[r, lot, dy - 1], bw_r.at[r, lot, dy - 1], at_y(dy))

    def fetch_copy(r, dy, g):
        first, rows = GROUPS[g] * CAP, (GROUPS[g + 1] - GROUPS[g]) * CAP
        return remote(
            ys.at[dy - 1, pl.ds(first, rows)], yrs[r].at[pl.ds(dy * COL + first, rows)],
            fw_s.at[r, g, dy - 1], fw_r.at[r, g, dy - 1], at_y(dy),
        )

    def sum_y_copy(n, dy):
        return remote(sp.at[n], sb.at[n, dy - 1], sy_s.at[n, dy - 1], sy_r.at[n, dy - 1], at_y(dy))

    def sum_z_copy(n, dz):
        return remote(sc.at[n], sd.at[n, dz - 1], sz_s.at[n, dz - 1], sz_r.at[n, dz - 1], at_z(dz))

    def core_copy(c):
        piece = pl.ds(c * CHUNK, CHUNK)
        return remote(cs.at[1 - core, :, piece], cp.at[:, piece], cp_s.at[c], cp_r.at[c], partner)

    def counts_copy(c, dx):
        piece = pl.ds(c * CHUNK, CHUNK)
        return remote(
            cx.at[lax.rem(x + dx, NX), piece], cr.at[dx - 1, piece], ct_s.at[c, dx - 1], ct_r.at[c, dx - 1], at_x(dx)
        )

    def sum_over_y(n):
        sp[n] = jnp.zeros((8, BS), F32)
        for m in range(2):
            sp[n, m : m + 1, :NS] = jnp.sum(sa[n, m].T, axis=0, keepdims=True)
        for dy in range(1, NY):
            sum_y_copy(n, dy).start()

    def sum_over_z(n):
        for dy in range(1, NY):
            sum_y_copy(n, dy).wait()
        sc[n] = sp[n] + sb[n, 0] + sb[n, 1] + sb[n, 2]
        for dz in range(1, NZ):
            sum_z_copy(n, dz).start()

    def sum_result(n):
        for dz in range(1, NZ):
            sum_z_copy(n, dz).wait()
        total = sc[n]
        for dz in range(1, NZ):
            total = total + sd[n, dz - 1]
        total = total / total_states
        return [jnp.broadcast_to(total[m : m + 1, :NS], (BS, NS)).T for m in range(2)]

    def weigh(r):
        u = STEPS - 1 - r

        def weigh_block(blocks, carry):
            for b in blocks:
                message = beta[:, cols(b)] if r == 0 else bacc[b]
                if r == 3:
                    message = message * scale[1]
                w[u, b] = (em[u, :, cols(b)].astype(F32) * message).astype(BF16)
            return carry

        loop(NB, weigh_block, 0, 4)

    def partials(r):
        u = STEPS - 1 - r

        def partial_block(js, acc):
            outs = [
                lax.dot_general(w[u, j], tr[j], (((1,), (1,)), ((), ())), preferred_element_type=F32) for j in js
            ]
            for j, out in zip(js, outs):
                for k in range(K):
                    piece = out[:, k * BS : (k + 1) * BS]
                    pb[j * K + k] = piece.astype(BF16)
                    if r >= 2:
                        acc = acc + piece
            return acc

        acc = loop(NB, partial_block, jnp.zeros((NS, BS), F32), 4)
        if r >= 2:
            sa[r - 2, 1] = acc

    def send_back(r, lot):
        first, past = LOTS[lot], LOTS[lot + 1]
        for dy in (1, 3, 2):

            def pack(turns, carry, dy=dy):
                for n in turns:
                    base = INV + dy * COL + n * CAP
                    values = [pb[tab[base + c]] for c in range(CAP)]
                    for c in range(CAP):
                        bsend[dy - 1, n, c] = values[c]
                return carry

            lax.fori_loop(first, past, lambda n, carry, pack=pack: pack([n], carry), 0)
            back_copy(r, dy, lot).start()

        def keep(turns, carry, lot=lot, first=first):
            for n in turns:
                base = INV + n * CAP
                values = [pb[tab[base + c]] for c in range(CAP)]
                for c in range(CAP):
                    brs[r % 2][lot][n - first, c] = values[c]
            return carry

        lax.fori_loop(first, past, lambda n, carry, keep=keep: keep([n], carry), 0)

    def relay(r, d):
        turn = TURNS.index(d % NZ)
        lot = sum(turn >= first for first in LOTS[1:-1])
        br, place = brs[r % 2][lot], turn - LOTS[lot]
        base = turn * NB
        pre[0] = jnp.zeros((NS, BS), F32)

        def add(numbers, acc):
            terms = [br[place, tab[ORD + base + i]] for i in numbers]
            for i, term in zip(numbers, terms):
                acc = acc + term.astype(F32)
                pre[i + 1] = acc
            return acc

        loop(NB, add, jnp.zeros((NS, BS), F32), 8)

        def differ(blocks, carry):
            values = [pre[tab[HI + base + b]] - pre[tab[LO + base + b]] for b in blocks]
            for b, value in zip(blocks, values):
                psv[d % NZ, b] = value
            return carry

        loop(NB, differ, 0, 4)

    def mix(r, c, acc):
        yr = yrs[r]

        def mix_block(numbers, acc):
            js = [c * PIECE + i for i in numbers]
            fetched = [jnp.concatenate([yr[tab[REF + j * K + k]] for k in range(K)], axis=1) for j in js]
            outs = [jnp.dot(f, tr[j], preferred_element_type=F32) for f, j in zip(fetched, js)]
            for j, out in zip(js, outs):
                value = out * em[r, :, cols(j)].astype(F32)
                if r == 3:
                    alpha_end[:, cols(j)] = value
                    acc = acc + value
                else:
                    zgs[(r + 1) % 2][0][j] = value.astype(BF16)
            return acc

        return loop(PIECE, mix_block, acc, 4)

    def choose(r, g):
        zg, yr = zgs[r % 2], yrs[r]
        for n in range(GROUPS[g], GROUPS[g + 1]):
            d = NEAR[n]
            base = SEL + d * CAP

            def choose_one(dy, carry, n=n, d=d, base=base):
                values = [zg[d][tab[base + dy * COL + c]] for c in range(CAP)]
                for c in range(CAP):
                    ys[dy - 1, n * CAP + c] = values[c]
                return carry

            lax.fori_loop(1, NY, choose_one, 0)
        for dy in (1, 3, 2):
            fetch_copy(r, dy, g).start()
        for n in range(GROUPS[g], GROUPS[g + 1]):
            values = [zg[NEAR[n]][tab[SEL + NEAR[n] * CAP + c]] for c in range(CAP)]
            for c in range(CAP):
                yr[n * CAP + c] = values[c]

    def pass_on(r, h):
        for c in range(PIECES):
            for way in range(2):
                gather_copy(r, way, h - 1, c).wait_recv()
                if h < 4 or travels(way, c):
                    gather_copy(r, way, h, c).start()

    def gather_end(r):
        for c in range(PIECES):
            gather_copy(r, 0 if travels(0, c) else 1, 4, c).wait_recv()

    def reduce_step(r, h):
        if h == 1:
            relay(r, 4)

            def far(blocks, carry):
                for b in blocks:
                    rs_snd[b] = psv[4, b].astype(BF16)
                return carry

            loop(NB, far, 0, 4)
            for c in range(PIECES):
                reduce_copy(r, 0 if travels(0, c) else 1, 1, c).start()
            return
        for way in range(2):
            relay(r, h - 5 if way else 5 - h)
        for c in range(PIECES):
            for way in range(2):
                d = (h - 5 if way else 5 - h) % NZ
                received = h > 2 or travels(way, c)
                if received:
                    reduce_copy(r, way, h - 1, c).wait_recv()

                def join(numbers, carry, way=way, d=d, c=c, received=received):
                    for b in [c * PIECE + i for i in numbers]:
                        value = psv[d, b]
                        if r == 3 and h == 4:
                            psv[d, b] = value + rl_rcv[way, 0, b]
                            continue
                        if received:
                            value = value + rs_rcv[r % 2, way, h - 2, b].astype(F32)
                        if r == 3 and h == 3:
                            psv[d, b] = value
                        else:
                            rs_rcv[r % 2, way, h - 2, b] = value.astype(BF16)
                    return carry

                loop(PIECE, join, 0, 4)
                reduce_copy(r, way, h, c).start()

    def reduce_end(r):
        acc = jnp.zeros((NS, BS), F32)
        for c in range(PIECES):
            for way in range(2):
                reduce_copy(r, way, 4, c).wait_recv()

            def finish(numbers, acc, c=c):
                for b in [c * PIECE + i for i in numbers]:
                    value = psv[0, b] + rs_rcv[r % 2, 0, 3, b].astype(F32) + rs_rcv[r % 2, 1, 3, b].astype(F32)
                    bacc[b] = value
                    if r == 1:
                        acc = acc + value * zgs[0][0][b].astype(F32)
                return acc

            acc = loop(PIECE, finish, acc, 4)
        if r == 1:
            sa[0, 0] = acc
        for way in range(2):
            for h in range(1, 5):
                for c in range(PIECES):
                    if h > 1 or travels(way, c):
                        reduce_copy(r, way, h, c).wait_send()

    loads[0].wait()
    for c in range(PIECES):

        def begin(numbers, carry, c=c):
            for b in [c * PIECE + i for i in numbers]:
                za0[b] = alpha[:, cols(b)].astype(BF16)
            return carry

        loop(PIECE, begin, 0, 4)
        if c == 0:
            pl.semaphore_wait(barrier, NZ - 1 + NY - 1 + NX)
        for way in range(2):
            gather_copy(0, way, 1, c).start()
    choose(0, 0)

    def emit(i, carry):
        span = pl.ds(pl.multiple_of(i * 256, 256), 256)
        rows = jnp.dot(hot[...], cols_in[:, span], preferred_element_type=F32).astype(BF16)
        for t in range(STEPS):
            em[t, :, span] = rows[t * NS : (t + 1) * NS]
        return carry

    loads[1].wait()
    lax.fori_loop(0, NB * BS // 256, emit, 0)
    loads[2].wait()
    weigh(0)
    loads[3].wait()
    partials(0)
    pass_on(0, 2)
    choose(0, 1)
    pass_on(0, 3)
    choose(0, 2)
    pass_on(0, 4)
    choose(0, 3)
    gather_end(0)
    choose(0, 4)

    def await_back(r, lot):
        for dy in range(1, NY):
            back_copy(r, dy, lot).wait()

    for r in range(STEPS):
        for g in range(len(GROUPS) - 1):
            if g == len(GROUPS) - 2:
                send_back(r, 0)
            for dy in range(1, NY):
                fetch_copy(r, dy, g).wait()
        for lot in range(1, len(LOTS) - 1):
            send_back(r, lot)
        for way in range(2):
            for h in range(1, 5):
                for c in range(PIECES):
                    if h < 4 or travels(way, c):
                        gather_copy(r, way, h, c).wait_send()
        if r == 2:
            sum_over_z(0)
        if r < 3:
            acc = jnp.zeros((NS, BS), F32)
            for c in range(PIECES):
                mix(r, c, acc)
                for way in range(2):
                    gather_copy(r + 1, way, 1, c).start()
            for h in range(2, 5):
                pass_on(r + 1, h)
            for g in range(3):
                choose(r + 1, g)
            await_back(r, 0)
            reduce_step(r, 1)
            choose(r + 1, 3)
            gather_end(r + 1)
            choose(r + 1, 4)
            reduce_step(r, 2)
            await_back(r, 1)
            reduce_step(r, 3)
            await_back(r, 2)
            reduce_step(r, 4)
            await_back(r, 3)
            relay(r, 0)
            reduce_end(r)
            if r == 2:
                means = sum_result(0)
                scale[0] = 1.0 / means[0]
                scale[1] = 1.0 / means[1]
                scale[2] = means[1] / means[0]
            weigh(r + 1)
            partials(r + 1)
            if r == 1:
                sum_over_y(0)

    def merge(c):
        core_copy(c).wait()

        def merge_block(i, carry):
            j = c * CHUNK + i
            for xp in range(NX):
                cx[xp, j] = (cs[core, xp, j] + cp[xp, j]).astype(BF16)
            return carry

        lax.fori_loop(0, CHUNK, merge_block, 0)
        for dx in range(1, NX):
            counts_copy(c, dx).start()

    for c in range(NB // CHUNK):

        def tally(i, carry, c=c):
            j = c * CHUNK + i
            left = jnp.concatenate(
                [jnp.concatenate([v[tab[REF + j * K + k]] for k in range(K)], axis=1) for v in yrs], axis=0
            )
            right = jnp.concatenate(
                [(w[t, j].astype(F32) * scale[2 if t == 0 else 0]).astype(BF16) for t in range(STEPS)], axis=0
            )
            out = lax.dot_general(left, right, (((0,), (0,)), ((), ())), preferred_element_type=F32)
            for k in range(K):
                for n in range(8):
                    first = k * BS + n * 16
                    cs[n % 2, n // 2, j, k] = out[first : first + 16]
            return carry

        lax.fori_loop(0, CHUNK, tally, 0)
        core_copy(c).start()

    acc = jnp.zeros((NS, BS), F32)
    for c in range(PIECES):
        acc = mix(3, c, acc)
    sa[1, 0] = acc
    sum_over_y(1)
    await_back(3, 0)
    reduce_step(3, 1)
    sum_over_z(1)
    reduce_step(3, 2)
    for c in range(NB // CHUNK):
        merge(c)
    await_back(3, 1)
    reduce_step(3, 3)
    await_back(3, 2)
    reduce_step(3, 4)
    await_back(3, 3)
    relay(3, 0)

    def total(c):
        for dx in range(1, NX):
            counts_copy(c, dx).wait()

        def total_block(i, carry):
            j = c * CHUNK + i
            value = cs[core, x, j] + cp[x, j]
            for dx in range(1, NX):
                value = value + cr[dx - 1, j].astype(F32)
            for k in range(K):
                rows = pl.ds(pl.multiple_of(k * BS + q * 16, 16), 16)
                counts[j, k] = value[k] * tr[j, rows, :].astype(F32)
            return carry

        lax.fori_loop(0, CHUNK, total_block, 0)

    means = sum_result(1)
    start_scale = 1.0 / means[1]
    end_scale = 1.0 / means[0]
    loglik[...] = jnp.log(means[0])

    def settle(b, carry):
        alpha_end[:, cols(b)] = alpha_end[:, cols(b)] * end_scale
        return carry

    lax.fori_loop(0, NB, settle, 0)
    for c in range(NB // CHUNK):
        total(c)
    for c in range(PIECES):
        for way in range(2):
            reduce_copy(3, way, 4, c).wait_recv()

        def last(i, carry, c=c):
            b = c * PIECE + i
            beta_start[:, cols(b)] = (psv[0, b] + rl_rcv[0, 1, b] + rl_rcv[1, 1, b]) * start_scale
            return carry

        lax.fori_loop(0, PIECE, last, 0)
    for way in range(2):
        for h in range(1, 5):
            for c in range(PIECES):
                if h > 1 or travels(way, c):
                    reduce_copy(3, way, h, c).wait_send()


def shards(alpha_in, beta_in, transitions, emission_cols, token_ids, sources):
    tables = index_tables(sources)
    hot = (token_ids.T.reshape(STEPS * NS, 1) == jnp.arange(TOKENS, dtype=jnp.int32)).astype(BF16)
    shard = (NB, NS, BS)
    vmem = pl.BlockSpec(memory_space=pltpu.VMEM)
    dma = pltpu.SemaphoreType.DMA
    out = pl.pallas_call(
        body,
        out_shape=(
            jax.ShapeDtypeStruct((NB, K, BS // 8, BS), F32),
            jax.ShapeDtypeStruct((NS, NB * BS), F32),
            jax.ShapeDtypeStruct((NS, NB * BS), F32),
            jax.ShapeDtypeStruct((NS, BS), F32),
        ),
        in_specs=[pl.BlockSpec(memory_space=pltpu.SMEM), vmem] + [pl.BlockSpec(memory_space=pl.ANY)] * 4,
        out_specs=(vmem,) * 4,
        scratch_shapes=[
            *[pltpu.VMEM(shard, BF16)] * (2 * NZ),
            pltpu.VMEM((STEPS, NS, NB * BS), BF16),
            *[pltpu.VMEM((NY * COL, NS, BS), BF16)] * STEPS,
            pltpu.VMEM((NY - 1, COL, NS, BS), BF16),
            pltpu.VMEM((REFS, NS, BS), BF16),
            pltpu.VMEM((NY - 1, NZ, CAP, NS, BS), BF16),
            *[pltpu.VMEM((LOTS[n + 1] - LOTS[n], NY * CAP, NS, BS), BF16) for n in (0, 1, 2, 3) * 2],
            pltpu.VMEM((NB + 1, NS, BS), F32),
            pltpu.VMEM((NZ,) + shard, F32),
            pltpu.VMEM(shard, BF16),
            pltpu.VMEM((2, 2, 4) + shard, BF16),
            pltpu.VMEM((2, 2) + shard, F32),
            pltpu.VMEM((STEPS,) + shard, BF16),
            pltpu.VMEM(shard, F32),
            pltpu.VMEM((2, NX, NB, K, BS // 8, BS), F32),
            pltpu.VMEM((NX, NB, K, BS // 8, BS), F32),
            pltpu.VMEM((NX, NB, K, BS // 8, BS), BF16),
            pltpu.VMEM((NX - 1, NB, K, BS // 8, BS), BF16),
            pltpu.VMEM((2, 2, NS, BS), F32),
            pltpu.VMEM((2, 8, BS), F32),
            pltpu.VMEM((2, NY - 1, 8, BS), F32),
            pltpu.VMEM((2, 8, BS), F32),
            pltpu.VMEM((2, NZ - 1, 8, BS), F32),
            pltpu.VMEM((3, NS, BS), F32),
            pltpu.VMEM((NS, NB * BS), F32),
            pltpu.VMEM((NS, NB * BS), F32),
            pltpu.VMEM((NB, K * BS, BS), BF16),
            pltpu.VMEM((TOKENS, NB * BS), BF16),
            dma((4,)),
            *[dma((STEPS, 2, 4, PIECES))] * 2,
            *[dma((STEPS, len(LOTS) - 1, NY - 1))] * 2,
            *[dma((STEPS, len(GROUPS) - 1, NY - 1))] * 2,
            *[dma((STEPS, 2, 4, PIECES))] * 2,
            *[dma((2, NY - 1))] * 2,
            *[dma((2, NZ - 1))] * 2,
            *[dma((NB // CHUNK,))] * 2,
            *[dma((NB // CHUNK, NX - 1))] * 2,
        ],
        compiler_params=pltpu.CompilerParams(
            collective_id=0, has_side_effects=True, vmem_limit_bytes=62 * 2**20
        ),
        cost_estimate=pl.CostEstimate(flops=1_700_000_000, bytes_accessed=10_000_000, transcendentals=32),
    )(tables, hot, alpha_in, beta_in, transitions.reshape(NB, K * BS, BS), emission_cols)
    return out[0], out[1], out[2], out[3][:, 0]


def solution(mesh):
    placed = (
        P("seq", "state"),
        P("seq", "state"),
        P("state", None, None, None),
        P(None, "state"),
        P("seq", None),
        P(),
    )
    return jax.shard_map(
        shards,
        mesh=mesh,
        in_specs=placed,
        out_specs=(P("state", None, "seq", None), P("seq", "state"), P("seq", "state"), P("seq")),
        check_vma=False,
    )
```

```python
import functools

import jax
import jax.numpy as jnp
from jax import lax
from jax.experimental import pallas as pl
from jax.experimental.pallas import tpu as pltpu
from jax.sharding import PartitionSpec as P

K = 4
STEPS = 4
NZ = 8
NY = 4
NX = 4
CAP = 8
NB = 32
NS = 32
BS = 128
REFS = NB * K
COL = NZ * CAP
CHUNK = 8
PIECES = 8
PIECE = NB // PIECES
TURNS = (4, 3, 5, 2, 6, 1, 7, 0)
LOTS = (0, 3, 5, 7, 8)
NEAR = (0, 1, 7, 2, 6, 3, 5, 4)
GROUPS = (0, 1, 3, 5, 7, 8)
TOKENS = 256
MESH = pl.DeviceIdType.MESH
F32 = jnp.float32
BF16 = jnp.bfloat16

SEL, REF, INV, ORD, LO, HI = 0, 256, 384, 640, 896, 1152


def index_tables(sources):
    rank = lax.axis_index("state")
    z, y = rank // NY, rank % NY
    rows = lax.dynamic_slice_in_dim(sources.reshape(NZ, NY * REFS), z, 1, 0).reshape(NY, REFS)
    rows = jnp.roll(rows, -y, axis=0)
    owner, local = rows // NB, rows % NB
    ordinal = jnp.arange(REFS, dtype=jnp.int32)
    earlier = (owner[:, None, :] == owner[:, :, None]) & (ordinal[None, :] < ordinal[:, None])[None]
    slot = jnp.sum(earlier.astype(jnp.int32), axis=2)
    ahead = (owner // NY - z) % NZ
    column = owner % NY
    place = ahead * CAP + slot
    spots = jnp.arange(COL, dtype=jnp.int32)
    mine = (column == y)[:, :, None] & (place[:, :, None] == spots)
    sel = jnp.sum(jnp.where(mine, local[:, :, None], 0), axis=1)
    filled = jnp.any(mine, axis=1)
    near = jnp.where(ahead[0] <= 3, jnp.maximum(2 * ahead[0] - 1, 0), jnp.minimum(16 - 2 * ahead[0], 7))
    ref = ((y - column[0]) % NY) * COL + near * CAP + slot[0]
    turn = jnp.where(ahead[0] <= 4, jnp.maximum(7 - 2 * ahead[0], 0), 2 * ahead[0] - 8)
    towards = ((column[0] - y) % NY) * COL + turn * CAP + slot[0]
    inv = jnp.sum(
        jnp.where(towards[:, None] == jnp.arange(NY * COL, dtype=jnp.int32), ordinal[:, None], 0), axis=0
    )
    key = jnp.where(filled, sel, NB)
    key = jnp.concatenate([key[:1], key[:0:-1]], axis=0).reshape(NY, NZ, CAP)
    key = key.transpose(1, 0, 2).reshape(NZ, NY * CAP)
    key = jnp.stack([key[d] for d in TURNS])
    number = jnp.arange(NY * CAP, dtype=jnp.int32)
    less = (key[:, None, :] < key[:, :, None]) | (
        (key[:, None, :] == key[:, :, None]) & (number[None, :] < number[:, None])[None]
    )
    rank_of = jnp.sum(less.astype(jnp.int32), axis=2)
    order = jnp.sum(jnp.where(rank_of[:, :, None] == number, number[None, :, None], 0), axis=1)
    blocks = jnp.arange(NB, dtype=jnp.int32)
    low = jnp.sum((key[:, None, :] < blocks[None, :, None]).astype(jnp.int32), axis=2)
    high = jnp.sum((key[:, None, :] <= blocks[None, :, None]).astype(jnp.int32), axis=2)
    return jnp.concatenate([part.reshape(-1).astype(jnp.int32) for part in (sel, ref, inv, order, low, high)])


def loop(count, fn, init=0, width=1):
    def several(i, carry):
        return fn([i * width + n for n in range(width)], carry)

    several.__name__ = fn.__name__
    return lax.fori_loop(0, count // width, several, init)


def body(
    tab, hot, alpha_hbm, beta_hbm, tr_hbm, cols_hbm,
    counts, alpha_end, beta_start, loglik,
    za0, za1, za2, za3, za4, za5, za6, za7, zb0, zb1, zb2, zb3, zb4, zb5, zb6, zb7,
    em, yr0, yr1, yr2, yr3, ys, pb, bsend, ba0, ba1, ba2, ba3, bb0, bb1, bb2, bb3, pre, psv,
    rs_snd, rs_rcv, rl_rcv, w, bacc, cs, cp, cx, cr, sa, sp, sb, sc, sd, scale, alpha, beta, tr, cols_in, ld,
    ag_s, ag_r, bw_s, bw_r, fw_s, fw_r, rs_s, rs_r, sy_s, sy_r, sz_s, sz_r, cp_s, cp_r, ct_s, ct_r,
):
    q, p = lax.axis_index("seq"), lax.axis_index("state")
    z, y = p // NY, p % NY
    x, core = q // 2, q % 2
    zgs = (za0, za1, za2, za3, za4, za5, za6, za7), (zb0, zb1, zb2, zb3, zb4, zb5, zb6, zb7)
    yrs, brs = (yr0, yr1, yr2, yr3), ((ba0, ba1, ba2, ba3), (bb0, bb1, bb2, bb3))
    total_states = float(NB * BS * NZ * NY)

    def at_z(dz):
        return (q, lax.rem(z + dz + NZ, NZ) * NY + y)

    def at_y(dy):
        return (q, z * NY + lax.rem(y + dy, NY))

    def at_x(dx):
        return (lax.rem(x + dx, NX) * 2 + core, p)

    partner = (x * 2 + 1 - core, p)

    loads = [
        pltpu.make_async_copy(src, dst, ld.at[n])
        for n, (src, dst) in enumerate(((alpha_hbm, alpha), (cols_hbm, cols_in), (beta_hbm, beta), (tr_hbm, tr)))
    ]
    for load in loads:
        load.start()
    barrier = pltpu.get_barrier_semaphore()
    for dz in range(1, NZ):
        pl.semaphore_signal(barrier, inc=1, device_id=at_z(dz), device_id_type=MESH)
    for dy in range(1, NY):
        pl.semaphore_signal(barrier, inc=1, device_id=at_y(dy), device_id_type=MESH)
    for dx in range(1, NX):
        pl.semaphore_signal(barrier, inc=1, device_id=at_x(dx), device_id_type=MESH)
    pl.semaphore_signal(barrier, inc=1, device_id=partner, device_id_type=MESH)

    def remote(src, dst, send, recv, device):
        return pltpu.make_async_remote_copy(
            src_ref=src, dst_ref=dst, send_sem=send, recv_sem=recv, device_id=device, device_id_type=MESH
        )

    def cols(j):
        return pl.ds(pl.multiple_of(j * BS, BS), BS)

    def part(c):
        return pl.ds(c * PIECE, PIECE)

    def travels(way, c):
        return c // (PIECES // 2) == way

    def gather_copy(r, way, h, c):
        zg = zgs[r % 2]
        near, far = (h - 1, h) if way else ((1 - h) % NZ, (-h) % NZ)
        return remote(
            zg[near].at[part(c)], zg[far].at[part(c)],
            ag_s.at[r, way, h - 1, c], ag_r.at[r, way, h - 1, c], at_z(-1 if way else 1),
        )

    def reduce_copy(r, way, h, c):
        if r == 3 and h >= 3:
            d = (h - 5 if way else 5 - h) % NZ
            src, dst = psv.at[d, part(c)], rl_rcv.at[way, h - 3, part(c)]
        else:
            src = rs_snd.at[part(c)] if h == 1 else rs_rcv.at[r % 2, way, h - 2, part(c)]
            dst = rs_rcv.at[r % 2, way, h - 1, part(c)]
        return remote(src, dst, rs_s.at[r, way, h - 1, c], rs_r.at[r, way, h - 1, c], at_z(-1 if way else 1))

    def back_copy(r, dy, lot):
        src = bsend.at[dy - 1, pl.ds(LOTS[lot], LOTS[lot + 1] - LOTS[lot])]
        dst = brs[r % 2][lot].at[:, pl.ds(dy * CAP, CAP)]
        return remote(src, dst, bw_s.at[r, lot, dy - 1], bw_r.at[r, lot, dy - 1], at_y(dy))

    def fetch_copy(r, dy, g):
        first, rows = GROUPS[g] * CAP, (GROUPS[g + 1] - GROUPS[g]) * CAP
        return remote(
            ys.at[dy - 1, pl.ds(first, rows)], yrs[r].at[pl.ds(dy * COL + first, rows)],
            fw_s.at[r, g, dy - 1], fw_r.at[r, g, dy - 1], at_y(dy),
        )

    def sum_y_copy(n, dy):
        return remote(sp.at[n], sb.at[n, dy - 1], sy_s.at[n, dy - 1], sy_r.at[n, dy - 1], at_y(dy))

    def sum_z_copy(n, dz):
        return remote(sc.at[n], sd.at[n, dz - 1], sz_s.at[n, dz - 1], sz_r.at[n, dz - 1], at_z(dz))

    def core_copy(c):
        piece = pl.ds(c * CHUNK, CHUNK)
        return remote(cs.at[1 - core, :, piece], cp.at[:, piece], cp_s.at[c], cp_r.at[c], partner)

    def counts_copy(c, dx):
        piece = pl.ds(c * CHUNK, CHUNK)
        return remote(
            cx.at[lax.rem(x + dx, NX), piece], cr.at[dx - 1, piece], ct_s.at[c, dx - 1], ct_r.at[c, dx - 1], at_x(dx)
        )

    def sum_over_y(n):
        sp[n] = jnp.zeros((8, BS), F32)
        for m in range(2):
            sp[n, m : m + 1, :NS] = jnp.sum(sa[n, m].T, axis=0, keepdims=True)
        for dy in range(1, NY):
            sum_y_copy(n, dy).start()

    def sum_over_z(n):
        for dy in range(1, NY):
            sum_y_copy(n, dy).wait()
        sc[n] = sp[n] + sb[n, 0] + sb[n, 1] + sb[n, 2]
        for dz in range(1, NZ):
            sum_z_copy(n, dz).start()

    def sum_result(n):
        for dz in range(1, NZ):
            sum_z_copy(n, dz).wait()
        total = sc[n]
        for dz in range(1, NZ):
            total = total + sd[n, dz - 1]
        total = total / total_states
        return [jnp.broadcast_to(total[m : m + 1, :NS], (BS, NS)).T for m in range(2)]

    def weigh(r):
        u = STEPS - 1 - r

        def weigh_block(blocks, carry):
            for b in blocks:
                message = beta[:, cols(b)] if r == 0 else bacc[b]
                if r == 3:
                    message = message * scale[1]
                w[u, b] = (em[u, :, cols(b)].astype(F32) * message).astype(BF16)
            return carry

        loop(NB, weigh_block, 0, 4)

    def partials(r):
        u = STEPS - 1 - r

        def partial_block(js, acc):
            outs = [
                lax.dot_general(w[u, j], tr[j], (((1,), (1,)), ((), ())), preferred_element_type=F32) for j in js
            ]
            for j, out in zip(js, outs):
                for k in range(K):
                    piece = out[:, k * BS : (k + 1) * BS]
                    pb[j * K + k] = piece.astype(BF16)
                    if r >= 2:
                        acc = acc + piece
            return acc

        acc = loop(NB, partial_block, jnp.zeros((NS, BS), F32), 4)
        if r >= 2:
            sa[r - 2, 1] = acc

    def send_back(r, lot):
        first, past = LOTS[lot], LOTS[lot + 1]
        for dy in (1, 3, 2):

            def pack(turns, carry, dy=dy):
                for n in turns:
                    base = INV + dy * COL + n * CAP
                    values = [pb[tab[base + c]] for c in range(CAP)]
                    for c in range(CAP):
                        bsend[dy - 1, n, c] = values[c]
                return carry

            lax.fori_loop(first, past, lambda n, carry, pack=pack: pack([n], carry), 0)
            back_copy(r, dy, lot).start()

        def keep(turns, carry, lot=lot, first=first):
            for n in turns:
                base = INV + n * CAP
                values = [pb[tab[base + c]] for c in range(CAP)]
                for c in range(CAP):
                    brs[r % 2][lot][n - first, c] = values[c]
            return carry

        lax.fori_loop(first, past, lambda n, carry, keep=keep: keep([n], carry), 0)

    def relay(r, d):
        turn = TURNS.index(d % NZ)
        lot = sum(turn >= first for first in LOTS[1:-1])
        br, place = brs[r % 2][lot], turn - LOTS[lot]
        base = turn * NB
        pre[0] = jnp.zeros((NS, BS), F32)

        def add(numbers, acc):
            terms = [br[place, tab[ORD + base + i]] for i in numbers]
            for i, term in zip(numbers, terms):
                acc = acc + term.astype(F32)
                pre[i + 1] = acc
            return acc

        loop(NB, add, jnp.zeros((NS, BS), F32), 8)

        def differ(blocks, carry):
            values = [pre[tab[HI + base + b]] - pre[tab[LO + base + b]] for b in blocks]
            for b, value in zip(blocks, values):
                psv[d % NZ, b] = value
            return carry

        loop(NB, differ, 0, 4)

    def mix(r, c, acc):
        yr = yrs[r]

        def mix_block(numbers, acc):
            js = [c * PIECE + i for i in numbers]
            fetched = [jnp.concatenate([yr[tab[REF + j * K + k]] for k in range(K)], axis=1) for j in js]
            outs = [jnp.dot(f, tr[j], preferred_element_type=F32) for f, j in zip(fetched, js)]
            for j, out in zip(js, outs):
                value = out * em[r, :, cols(j)].astype(F32)
                if r == 3:
                    alpha_end[:, cols(j)] = value
                    acc = acc + value
                else:
                    zgs[(r + 1) % 2][0][j] = value.astype(BF16)
            return acc

        return loop(PIECE, mix_block, acc, 4)

    def choose(r, g):
        zg, yr = zgs[r % 2], yrs[r]
        for n in range(GROUPS[g], GROUPS[g + 1]):
            d = NEAR[n]
            base = SEL + d * CAP

            def choose_one(dy, carry, n=n, d=d, base=base):
                values = [zg[d][tab[base + dy * COL + c]] for c in range(CAP)]
                for c in range(CAP):
                    ys[dy - 1, n * CAP + c] = values[c]
                return carry

            lax.fori_loop(1, NY, choose_one, 0)
        for dy in (1, 3, 2):
            fetch_copy(r, dy, g).start()
        for n in range(GROUPS[g], GROUPS[g + 1]):
            values = [zg[NEAR[n]][tab[SEL + NEAR[n] * CAP + c]] for c in range(CAP)]
            for c in range(CAP):
                yr[n * CAP + c] = values[c]

    def pass_on(r, h):
        for c in range(PIECES):
            for way in range(2):
                gather_copy(r, way, h - 1, c).wait_recv()
                if h < 4 or travels(way, c):
                    gather_copy(r, way, h, c).start()

    def gather_end(r):
        for c in range(PIECES):
            gather_copy(r, 0 if travels(0, c) else 1, 4, c).wait_recv()

    def reduce_step(r, h):
        if h == 1:
            relay(r, 4)

            def far(blocks, carry):
                for b in blocks:
                    rs_snd[b] = psv[4, b].astype(BF16)
                return carry

            loop(NB, far, 0, 4)
            for c in range(PIECES):
                reduce_copy(r, 0 if travels(0, c) else 1, 1, c).start()
            return
        for way in range(2):
            relay(r, h - 5 if way else 5 - h)
        for c in range(PIECES):
            for way in range(2):
                d = (h - 5 if way else 5 - h) % NZ
                received = h > 2 or travels(way, c)
                if received:
                    reduce_copy(r, way, h - 1, c).wait_recv()

                def join(numbers, carry, way=way, d=d, c=c, received=received):
                    for b in [c * PIECE + i for i in numbers]:
                        value = psv[d, b]
                        if r == 3 and h == 4:
                            psv[d, b] = value + rl_rcv[way, 0, b]
                            continue
                        if received:
                            value = value + rs_rcv[r % 2, way, h - 2, b].astype(F32)
                        if r == 3 and h == 3:
                            psv[d, b] = value
                        else:
                            rs_rcv[r % 2, way, h - 2, b] = value.astype(BF16)
                    return carry

                loop(PIECE, join, 0, 4)
                reduce_copy(r, way, h, c).start()

    def reduce_end(r):
        acc = jnp.zeros((NS, BS), F32)
        for c in range(PIECES):
            for way in range(2):
                reduce_copy(r, way, 4, c).wait_recv()

            def finish(numbers, acc, c=c):
                for b in [c * PIECE + i for i in numbers]:
                    value = psv[0, b] + rs_rcv[r % 2, 0, 3, b].astype(F32) + rs_rcv[r % 2, 1, 3, b].astype(F32)
                    bacc[b] = value
                    if r == 1:
                        acc = acc + value * zgs[0][0][b].astype(F32)
                return acc

            acc = loop(PIECE, finish, acc, 4)
        if r == 1:
            sa[0, 0] = acc
        for way in range(2):
            for h in range(1, 5):
                for c in range(PIECES):
                    if h > 1 or travels(way, c):
                        reduce_copy(r, way, h, c).wait_send()

    loads[0].wait()
    for c in range(PIECES):

        def begin(numbers, carry, c=c):
            for b in [c * PIECE + i for i in numbers]:
                za0[b] = alpha[:, cols(b)].astype(BF16)
            return carry

        loop(PIECE, begin, 0, 4)
        if c == 0:
            pl.semaphore_wait(barrier, NZ - 1 + NY - 1 + NX)
        for way in range(2):
            gather_copy(0, way, 1, c).start()
    choose(0, 0)

    def emit(i, carry):
        span = pl.ds(pl.multiple_of(i * 256, 256), 256)
        rows = jnp.dot(hot[...], cols_in[:, span], preferred_element_type=F32).astype(BF16)
        for t in range(STEPS):
            em[t, :, span] = rows[t * NS : (t + 1) * NS]
        return carry

    loads[1].wait()
    lax.fori_loop(0, NB * BS // 256, emit, 0)
    loads[2].wait()
    weigh(0)
    loads[3].wait()
    partials(0)
    pass_on(0, 2)
    choose(0, 1)
    pass_on(0, 3)
    choose(0, 2)
    pass_on(0, 4)
    choose(0, 3)
    gather_end(0)
    choose(0, 4)

    def await_back(r, lot):
        for dy in range(1, NY):
            back_copy(r, dy, lot).wait()

    for r in range(STEPS):
        for g in range(len(GROUPS) - 1):
            if g == len(GROUPS) - 2:
                send_back(r, 0)
            for dy in range(1, NY):
                fetch_copy(r, dy, g).wait()
        for lot in range(1, len(LOTS) - 1):
            send_back(r, lot)
        for way in range(2):
            for h in range(1, 5):
                for c in range(PIECES):
                    if h < 4 or travels(way, c):
                        gather_copy(r, way, h, c).wait_send()
        if r == 2:
            sum_over_z(0)
        if r < 3:
            acc = jnp.zeros((NS, BS), F32)
            for c in range(PIECES):
                mix(r, c, acc)
                for way in range(2):
                    gather_copy(r + 1, way, 1, c).start()
            for h in range(2, 5):
                pass_on(r + 1, h)
            for g in range(3):
                choose(r + 1, g)
            await_back(r, 0)
            reduce_step(r, 1)
            choose(r + 1, 3)
            gather_end(r + 1)
            choose(r + 1, 4)
            reduce_step(r, 2)
            await_back(r, 1)
            reduce_step(r, 3)
            await_back(r, 2)
            reduce_step(r, 4)
            await_back(r, 3)
            relay(r, 0)
            reduce_end(r)
            if r == 2:
                means = sum_result(0)
                scale[0] = 1.0 / means[0]
                scale[1] = 1.0 / means[1]
                scale[2] = means[1] / means[0]
            weigh(r + 1)
            partials(r + 1)
            if r == 1:
                sum_over_y(0)

    def merge(c):
        core_copy(c).wait()

        def merge_block(i, carry):
            j = c * CHUNK + i
            for xp in range(NX):
                cx[xp, j] = (cs[core, xp, j] + cp[xp, j]).astype(BF16)
            return carry

        lax.fori_loop(0, CHUNK, merge_block, 0)
        for dx in range(1, NX):
            counts_copy(c, dx).start()

    for c in range(NB // CHUNK):

        def tally(i, carry, c=c):
            j = c * CHUNK + i
            left = jnp.concatenate(
                [jnp.concatenate([v[tab[REF + j * K + k]] for k in range(K)], axis=1) for v in yrs], axis=0
            )
            right = jnp.concatenate(
                [(w[t, j].astype(F32) * scale[2 if t == 0 else 0]).astype(BF16) for t in range(STEPS)], axis=0
            )
            out = lax.dot_general(left, right, (((0,), (0,)), ((), ())), preferred_element_type=F32)
            for k in range(K):
                for n in range(8):
                    first = k * BS + n * 16
                    cs[n % 2, n // 2, j, k] = out[first : first + 16]
            return carry

        lax.fori_loop(0, CHUNK, tally, 0)
        core_copy(c).start()

    acc = jnp.zeros((NS, BS), F32)
    for c in range(PIECES):
        acc = mix(3, c, acc)
    sa[1, 0] = acc
    sum_over_y(1)
    await_back(3, 0)
    reduce_step(3, 1)
    sum_over_z(1)
    reduce_step(3, 2)
    for c in range(NB // CHUNK):
        merge(c)
    await_back(3, 1)
    reduce_step(3, 3)
    await_back(3, 2)
    reduce_step(3, 4)
    await_back(3, 3)
    relay(3, 0)

    def total(c):
        for dx in range(1, NX):
            counts_copy(c, dx).wait()

        def total_block(i, carry):
            j = c * CHUNK + i
            value = cs[core, x, j] + cp[x, j]
            for dx in range(1, NX):
                value = value + cr[dx - 1, j].astype(F32)
            for k in range(K):
                rows = pl.ds(pl.multiple_of(k * BS + q * 16, 16), 16)
                counts[j, k] = value[k] * tr[j, rows, :].astype(F32)
            return carry

        lax.fori_loop(0, CHUNK, total_block, 0)

    means = sum_result(1)
    start_scale = 1.0 / means[1]
    end_scale = 1.0 / means[0]
    loglik[...] = jnp.log(means[0])

    def settle(b, carry):
        alpha_end[:, cols(b)] = alpha_end[:, cols(b)] * end_scale
        return carry

    lax.fori_loop(0, NB, settle, 0)
    for c in range(NB // CHUNK):
        total(c)
    for c in range(PIECES):
        for way in range(2):
            reduce_copy(3, way, 4, c).wait_recv()

        def last(i, carry, c=c):
            b = c * PIECE + i
            beta_start[:, cols(b)] = (psv[0, b] + rl_rcv[0, 1, b] + rl_rcv[1, 1, b]) * start_scale
            return carry

        lax.fori_loop(0, PIECE, last, 0)
    for way in range(2):
        for h in range(1, 5):
            for c in range(PIECES):
                if h > 1 or travels(way, c):
                    reduce_copy(3, way, h, c).wait_send()


def shards(alpha_in, beta_in, transitions, emission_cols, token_ids, sources):
    tables = index_tables(sources)
    hot = (token_ids.T.reshape(STEPS * NS, 1) == jnp.arange(TOKENS, dtype=jnp.int32)).astype(BF16)
    shard = (NB, NS, BS)
    vmem = pl.BlockSpec(memory_space=pltpu.VMEM)
    dma = pltpu.SemaphoreType.DMA
    out = pl.pallas_call(
        body,
        out_shape=(
            jax.ShapeDtypeStruct((NB, K, BS // 8, BS), F32),
            jax.ShapeDtypeStruct((NS, NB * BS), F32),
            jax.ShapeDtypeStruct((NS, NB * BS), F32),
            jax.ShapeDtypeStruct((NS, BS), F32),
        ),
        in_specs=[pl.BlockSpec(memory_space=pltpu.SMEM), vmem] + [pl.BlockSpec(memory_space=pl.ANY)] * 4,
        out_specs=(vmem,) * 4,
        scratch_shapes=[
            *[pltpu.VMEM(shard, BF16)] * (2 * NZ),
            pltpu.VMEM((STEPS, NS, NB * BS), BF16),
            *[pltpu.VMEM((NY * COL, NS, BS), BF16)] * STEPS,
            pltpu.VMEM((NY - 1, COL, NS, BS), BF16),
            pltpu.VMEM((REFS, NS, BS), BF16),
            pltpu.VMEM((NY - 1, NZ, CAP, NS, BS), BF16),
            *[pltpu.VMEM((LOTS[n + 1] - LOTS[n], NY * CAP, NS, BS), BF16) for n in (0, 1, 2, 3) * 2],
            pltpu.VMEM((NB + 1, NS, BS), F32),
            pltpu.VMEM((NZ,) + shard, F32),
            pltpu.VMEM(shard, BF16),
            pltpu.VMEM((2, 2, 4) + shard, BF16),
            pltpu.VMEM((2, 2) + shard, F32),
            pltpu.VMEM((STEPS,) + shard, BF16),
            pltpu.VMEM(shard, F32),
            pltpu.VMEM((2, NX, NB, K, BS // 8, BS), F32),
            pltpu.VMEM((NX, NB, K, BS // 8, BS), F32),
            pltpu.VMEM((NX, NB, K, BS // 8, BS), BF16),
            pltpu.VMEM((NX - 1, NB, K, BS // 8, BS), BF16),
            pltpu.VMEM((2, 2, NS, BS), F32),
            pltpu.VMEM((2, 8, BS), F32),
            pltpu.VMEM((2, NY - 1, 8, BS), F32),
            pltpu.VMEM((2, 8, BS), F32),
            pltpu.VMEM((2, NZ - 1, 8, BS), F32),
            pltpu.VMEM((3, NS, BS), F32),
            pltpu.VMEM((NS, NB * BS), F32),
            pltpu.VMEM((NS, NB * BS), F32),
            pltpu.VMEM((NB, K * BS, BS), BF16),
            pltpu.VMEM((TOKENS, NB * BS), BF16),
            dma((4,)),
            *[dma((STEPS, 2, 4, PIECES))] * 2,
            *[dma((STEPS, len(LOTS) - 1, NY - 1))] * 2,
            *[dma((STEPS, len(GROUPS) - 1, NY - 1))] * 2,
            *[dma((STEPS, 2, 4, PIECES))] * 2,
            *[dma((2, NY - 1))] * 2,
            *[dma((2, NZ - 1))] * 2,
            *[dma((NB // CHUNK,))] * 2,
            *[dma((NB // CHUNK, NX - 1))] * 2,
        ],
        compiler_params=pltpu.CompilerParams(
            collective_id=0, has_side_effects=True, vmem_limit_bytes=62 * 2**20
        ),
        cost_estimate=pl.CostEstimate(flops=1_700_000_000, bytes_accessed=10_000_000, transcendentals=32),
    )(tables, hot, alpha_in, beta_in, transitions.reshape(NB, K * BS, BS), emission_cols)
    return out[0], out[1], out[2], out[3][:, 0]


def solution(mesh):
    placed = (
        P("seq", "state"),
        P("seq", "state"),
        P("state", None, None, None),
        P(None, "state"),
        P("seq", None),
        P(),
    )
    return jax.shard_map(
        shards,
        mesh=mesh,
        in_specs=placed,
        out_specs=(P("state", None, "seq", None), P("seq", "state"), P("seq", "state"), P("seq")),
        check_vma=False,
    )
```
